32 devices in a mesh: row: 4 (over z), col: 8 (over y, x, core).
Axes of the slice: x: 2, y: 2, z: 4, core: 2. Of those that a mesh axis runs over, the one named last changes fastest.
Arguments:
- field_in: float32 [16, 32, 64, 4], P(None, 'row', 'col'), may hold values from -6 to 6
- conv_weight: float32 [3, 3, 4, 256], replicated, may hold values from -1 to 1
- conv_bias: float32 [256], replicated, may hold values from -3 to 3
- first_gain: float32 [256], replicated, may hold values from 0.5 to 1.5
- first_shift: float32 [256], replicated, may hold values from -3 to 3
- query_weight: float32 [256, 256], replicated, may hold values from -0.375 to 0.375
- key_weight: float32 [256, 256], replicated, may hold values from -0.375 to 0.375
- value_weight: float32 [256, 256], replicated, may hold values from -0.375 to 0.375
- output_weight: float32 [256, 256], replicated, may hold values from -1 to 1
- second_gain: float32 [256], replicated, may hold values from 0.5 to 1.5
- second_shift: float32 [256], replicated, may hold values from -3 to 3
- hidden_weight: float32 [256, 512], replicated, may hold values from -0.375 to 0.375
- hidden_bias: float32 [512], replicated, may hold values from -3 to 3
- return_weight: float32 [512, 256], replicated, may hold values from -0.25 to 0.25
- return_bias: float32 [256], replicated, may hold values from -3 to 3
- decode_query: float32 [128, 256], replicated, may hold values from -0.5 to 0.5
- decode_key: float32 [256, 256], replicated, may hold values from -0.375 to 0.375
- decode_value: float32 [256, 256], replicated, may hold values from -0.375 to 0.375
- decode_output: float32 [256, 256], replicated, may hold values from -1 to 1
- propagate_up: float32 [256, 512], replicated, may hold values from -0.375 to 0.375
- propagate_bias: float32 [512], replicated, may hold values from -3 to 3
- propagate_down: float32 [512, 256], replicated, may hold values from -0.25 to 0.25
- propagate_shift: float32 [256], replicated, may hold values from -3 to 3
- cotangent: float32 [16, 32, 64, 256], P(None, 'row', 'col'), may hold values from -6 to 6
- grid_sizes: int32 [16, 2], replicated, may hold values from 16 to 64, as said below
Outputs:
- result_field: float32 [16, 32, 64, 256], P(None, 'row', 'col')
- field_grad: float32 [16, 32, 64, 4], P(None, 'row', 'col')
- conv_weight_grad: float32 [3, 3, 4, 256], replicated
- conv_bias_grad: float32 [256], replicated
- first_gain_grad: float32 [256], replicated
- first_shift_grad: float32 [256], replicated
- query_weight_grad: float32 [256, 256], replicated
- key_weight_grad: float32 [256, 256], replicated
- value_weight_grad: float32 [256, 256], replicated
- output_weight_grad: float32 [256, 256], replicated
- second_gain_grad: float32 [256], replicated
- second_shift_grad: float32 [256], replicated
- hidden_weight_grad: float32 [256, 512], replicated
- hidden_bias_grad: float32 [512], replicated
- return_weight_grad: float32 [512, 256], replicated
- return_bias_grad: float32 [256], replicated
- decode_query_grad: float32 [128, 256], replicated
- decode_key_grad: float32 [256, 256], replicated
- decode_value_grad: float32 [256, 256], replicated
- decode_output_grad: float32 [256, 256], replicated
- propagate_up_grad: float32 [256, 512], replicated
- propagate_bias_grad: float32 [512], replicated
- propagate_down_grad: float32 [512, 256], replicated
- propagate_shift_grad: float32 [256], replicated
The draws below stay inside these ranges and needn't reach their ends.
Inputs may be any that keep to these rules, and one draw needn't show every extreme that they name: `grid_sizes`: each item's valid rows are at most 32 and valid columns at most 64; in every draw one item covers the whole padded grid.
All inputs are finite; a program needn't handle non-finite values.
Results may differ from the reference program's by a relative error of at most 0.0003.
Values sent between devices are 32-bit elements; how exact they have to be, the bound alone decides.
A program may use at most 192 MiB of HBM per device.

```python
import math
import jax
import jax.numpy as jnp
from jax import lax

HEADS = 8
HEAD = 32
D = 256
FF = 512
FOUR = 128
CIN = 4
ITEMS = 16
NH = 32
NW = 64


def draw_grid_sizes(key, part):
    key = jax.random.fold_in(key, 7)
    key_rows, key_cols, key_pick = jax.random.split(key, 3)
    size_rows = jax.random.randint(key_rows, (ITEMS,), NH // 2, NH + 1)
    size_cols = jax.random.randint(key_cols, (ITEMS,), NW // 2, NW + 1)
    chosen = jax.random.randint(key_pick, (), 0, ITEMS)
    whole = jnp.arange(ITEMS) == chosen
    size_rows = jnp.where(whole, NH, size_rows)
    size_cols = jnp.where(whole, NW, size_cols)
    return jnp.stack([size_rows, size_cols], axis=1).astype(jnp.int32)


def level_of(key, extent, shards, smallest, top_value):
    loudness = 1.0
    for dim, blocks in shards:
        steps = jax.random.uniform(jax.random.fold_in(jax.random.fold_in(key, 6), dim), (blocks,), jnp.float32, smallest / len(shards), top_value / len(shards))
        loudness = loudness * jnp.repeat(jnp.exp(steps), extent[dim] // blocks).reshape((-1,) + (1,) * (len(extent) - 1 - dim))
    return loudness


def normal_values(stream_key, shape, width, limit, cuts=(), kind=jnp.bfloat16):
    values = width * jax.random.normal(stream_key, shape, jnp.float32)
    if cuts:
        values = values * level_of(stream_key, shape, cuts, -0.22, 0.18)
    return jnp.clip(values, -limit, limit).astype(kind)


def setup_inputs(seed: int = 0) -> dict:
    keys = jax.random.split(jax.random.key(seed), 26)
    field_in = normal_values(keys[0], (ITEMS, NH, NW, CIN), 1.0, 6.0, ((1, 4), (2, 8)), jnp.float32)
    conv_weight = normal_values(keys[1], (3, 3, CIN, D), (9 * CIN) ** -0.5, 1.0, (), jnp.float32)
    conv_bias = normal_values(keys[2], (D,), 0.5, 3.0, (), jnp.float32)
    first_gain = jnp.clip(1.0 + 0.1 * jax.random.normal(keys[3], (D,), jnp.float32), 0.5, 1.5)
    first_shift = normal_values(keys[4], (D,), 0.5, 3.0, (), jnp.float32)
    query_weight = normal_values(keys[5], (D, D), D ** -0.5, 0.375, (), jnp.float32)
    key_weight = normal_values(keys[6], (D, D), D ** -0.5, 0.375, (), jnp.float32)
    value_weight = normal_values(keys[7], (D, D), D ** -0.5, 0.375, (), jnp.float32)
    output_weight = normal_values(keys[8], (D, D), HEAD ** -0.5, 1.0, (), jnp.float32)
    second_gain = jnp.clip(1.0 + 0.1 * jax.random.normal(keys[9], (D,), jnp.float32), 0.5, 1.5)
    second_shift = normal_values(keys[10], (D,), 0.5, 3.0, (), jnp.float32)
    hidden_weight = normal_values(keys[11], (D, FF), D ** -0.5, 0.375, (), jnp.float32)
    hidden_bias = normal_values(keys[12], (FF,), 0.5, 3.0, (), jnp.float32)
    return_weight = normal_values(keys[13], (FF, D), FF ** -0.5, 0.25, (), jnp.float32)
    return_bias = normal_values(keys[14], (D,), 0.5, 3.0, (), jnp.float32)
    decode_query = normal_values(keys[15], (FOUR, D), FOUR ** -0.5, 0.5, (), jnp.float32)
    decode_key = normal_values(keys[16], (D, D), D ** -0.5, 0.375, (), jnp.float32)
    decode_value = normal_values(keys[17], (D, D), D ** -0.5, 0.375, (), jnp.float32)
    decode_output = normal_values(keys[18], (D, D), HEAD ** -0.5, 1.0, (), jnp.float32)
    propagate_up = normal_values(keys[19], (D, FF), D ** -0.5, 0.375, (), jnp.float32)
    propagate_bias = normal_values(keys[20], (FF,), 0.5, 3.0, (), jnp.float32)
    propagate_down = normal_values(keys[21], (FF, D), FF ** -0.5, 0.25, (), jnp.float32)
    propagate_shift = normal_values(keys[22], (D,), 0.5, 3.0, (), jnp.float32)
    cotangent = normal_values(keys[23], (ITEMS, NH, NW, D), 1.0, 6.0, ((1, 4), (2, 8)), jnp.float32)
    grid_sizes = draw_grid_sizes(jax.random.fold_in(keys[25], 71), 0)
    return dict(field_in=field_in, conv_weight=conv_weight, conv_bias=conv_bias, first_gain=first_gain, first_shift=first_shift, query_weight=query_weight, key_weight=key_weight, value_weight=value_weight, output_weight=output_weight, second_gain=second_gain, second_shift=second_shift, hidden_weight=hidden_weight, hidden_bias=hidden_bias, return_weight=return_weight, return_bias=return_bias, decode_query=decode_query, decode_key=decode_key, decode_value=decode_value, decode_output=decode_output, propagate_up=propagate_up, propagate_bias=propagate_bias, propagate_down=propagate_down, propagate_shift=propagate_shift, cotangent=cotangent, grid_sizes=grid_sizes)


@jax.custom_vjp
def low(v):
    return lax.optimization_barrier(v.astype(jnp.bfloat16)).astype(jnp.float32)

@jax.custom_vjp
def low_back(v):
    return v

def low_keep(v):
    return (low(v), None)

def low_pass(kept, grad):
    return (grad,)

def back_keep(v):
    return (v, None)

def back_low(kept, grad):
    return (low(grad),)
low.defvjp(low_keep, low_pass)
low_back.defvjp(back_keep, back_low)
highest = lax.Precision.HIGHEST

def matmul(left, right):
    return jnp.matmul(left, right, precision=highest)

def smooth(values):
    return jax.nn.gelu(values, approximate=True)

def layer_norm(values, norm_gain, norm_shift):
    average = lax.optimization_barrier(jnp.mean(values, axis=-1, keepdims=True))
    center = values - average
    spread = lax.optimization_barrier(jnp.mean(center * center, axis=-1, keepdims=True))
    return center * lax.rsqrt(spread + 1e-05) * norm_gain + norm_shift

def geometry(row_index, col_index, grid_sizes):
    size_rows = grid_sizes[:, 0]
    size_cols = grid_sizes[:, 1]
    within = (row_index[None, :, None] < size_rows[:, None, None]) & (col_index[None, None, :] < size_cols[:, None, None])
    inside = within.astype(jnp.float32)
    coord_x = (row_index.astype(jnp.float32)[None, :, None] + 0.5) / size_rows.astype(jnp.float32)[:, None, None] + 0.0 * inside
    coord_y = (col_index.astype(jnp.float32)[None, None, :] + 0.5) / size_cols.astype(jnp.float32)[:, None, None] + 0.0 * inside
    points = (size_rows * size_cols).astype(jnp.float32)
    return (inside, coord_x, coord_y, points)

def features(coord_x, coord_y):
    angles = math.pi * (jnp.arange(FOUR // 4).astype(jnp.float32) + 1.0)
    along_x = coord_x[..., None] * angles
    along_y = coord_y[..., None] * angles
    return jnp.concatenate([jnp.sin(along_x), jnp.cos(along_x), jnp.sin(along_y), jnp.cos(along_y)], axis=-1)

def rotate(vectors, coord_x, coord_y):
    quarter = HEAD // 4
    angles = 2.0 * math.pi * (jnp.arange(quarter).astype(jnp.float32) + 1.0)
    turn_x = coord_x[..., None, None] * angles
    turn_y = coord_y[..., None, None] * angles
    cosine_x, sine_x = (jnp.cos(turn_x), jnp.sin(turn_x))
    cosine_y, sine_y = (jnp.cos(turn_y), jnp.sin(turn_y))
    part_one = vectors[..., :quarter]
    part_two = vectors[..., quarter:2 * quarter]
    part_three = vectors[..., 2 * quarter:3 * quarter]
    part_four = vectors[..., 3 * quarter:]
    return jnp.concatenate([part_one * cosine_x - part_two * sine_x, part_one * sine_x + part_two * cosine_x, part_three * cosine_y - part_four * sine_y, part_three * sine_y + part_four * cosine_y], axis=-1)

def split_heads(values):
    return values.reshape(values.shape[:-1] + (HEADS, HEAD))

def conv_embed(padded, weight_in, bias_in):
    tile_rows = padded.shape[1] - 2
    tile_cols = padded.shape[2] - 2
    total = jnp.zeros(padded.shape[:1] + (tile_rows, tile_cols, weight_in.shape[-1]), jnp.float32)
    for shift_row in range(3):
        for shift_col in range(3):
            window = padded[:, shift_row:shift_row + tile_rows, shift_col:shift_col + tile_cols, :]
            total = total + jnp.einsum('brci,io->brco', window, weight_in[shift_row, shift_col], precision=highest)
    return total + bias_in

def project(params, hidden0, coord_x, coord_y):
    first_gain, first_shift, query_weight, key_weight, value_weight = params
    normed = layer_norm(hidden0, first_gain, first_shift)
    query_heads = rotate(split_heads(matmul(normed, query_weight)), coord_x, coord_y)
    key_heads = rotate(split_heads(matmul(normed, key_weight)), coord_x, coord_y)
    value_heads = split_heads(matmul(normed, value_weight))
    return (query_heads, key_heads, value_heads)

def summary(key_heads, value_heads, weight):
    return jnp.einsum('brchd,brche->bhde', key_heads * weight[..., None, None], value_heads, precision=highest)

def encoder_rest(params, hidden0, query_heads, kv_summary):
    output_weight, second_gain, second_shift, hidden_weight, hidden_bias, return_weight, return_bias = params
    mixed = jnp.einsum('brchd,bhde->brche', query_heads, kv_summary, precision=highest).reshape(hidden0.shape)
    hidden1 = hidden0 + matmul(mixed, output_weight)
    normed = layer_norm(hidden1, second_gain, second_shift)
    return hidden1 + matmul(smooth(matmul(normed, hidden_weight) + hidden_bias), return_weight) + return_bias

def decode_summary(params, hidden2, weight):
    decode_key, decode_value = params
    return summary(split_heads(matmul(hidden2, decode_key)), split_heads(matmul(hidden2, decode_value)), weight)

def decode_out(params, fourier, dec_summary, inside):
    decode_query, decode_output, propagate_up, propagate_bias, propagate_down, propagate_shift = params
    query_heads = split_heads(matmul(fourier, decode_query))
    mixed = jnp.einsum('brchd,bhde->brche', query_heads, dec_summary, precision=highest)
    latent = matmul(mixed.reshape(mixed.shape[:-2] + (HEADS * HEAD,)), decode_output)
    result = latent + matmul(smooth(matmul(latent, propagate_up) + propagate_bias), propagate_down) + propagate_shift
    return result * inside[..., None]

def forward(field, params, inside, coord_x, coord_y, points, fourier):
    conv_weight, conv_bias, first_gain, first_shift, query_weight, key_weight, value_weight, output_weight, second_gain, second_shift, hidden_weight, hidden_bias, return_weight, return_bias, decode_query, decode_key, decode_value, decode_output, propagate_up, propagate_bias, propagate_down, propagate_shift = params
    padded = jnp.pad(field * inside[..., None], ((0, 0), (1, 1), (1, 1), (0, 0)))
    hidden0 = conv_embed(padded, conv_weight, conv_bias)
    query_heads, key_heads, value_heads = project((first_gain, first_shift, query_weight, key_weight, value_weight), hidden0, coord_x, coord_y)
    weight = inside / points[:, None, None]
    kv_summary = summary(key_heads, value_heads, weight)
    hidden2 = encoder_rest((output_weight, second_gain, second_shift, hidden_weight, hidden_bias, return_weight, return_bias), hidden0, query_heads, kv_summary)
    dec_summary = decode_summary((decode_key, decode_value), hidden2, weight)
    return decode_out((decode_query, decode_output, propagate_up, propagate_bias, propagate_down, propagate_shift), fourier, dec_summary, inside)

def reference(field_in, conv_weight, conv_bias, first_gain, first_shift, query_weight, key_weight, value_weight, output_weight, second_gain, second_shift, hidden_weight, hidden_bias, return_weight, return_bias, decode_query, decode_key, decode_value, decode_output, propagate_up, propagate_bias, propagate_down, propagate_shift, cotangent, grid_sizes):
    row_index = jnp.arange(NH).astype(jnp.int32)
    col_index = jnp.arange(NW).astype(jnp.int32)
    inside, coord_x, coord_y, points = geometry(row_index, col_index, grid_sizes)
    fourier = features(coord_x, coord_y)
    params = (conv_weight, conv_bias, first_gain, first_shift, query_weight, key_weight, value_weight, output_weight, second_gain, second_shift, hidden_weight, hidden_bias, return_weight, return_bias, decode_query, decode_key, decode_value, decode_output, propagate_up, propagate_bias, propagate_down, propagate_shift)

    def run_layer(field, weights):
        return forward(field, weights, inside, coord_x, coord_y, points, fourier)
    result, back_fn = jax.vjp(run_layer, field_in, params)
    field_grad, grads = back_fn(cotangent)
    return (result, field_grad, grads[0], grads[1], grads[2], grads[3], grads[4], grads[5], grads[6], grads[7], grads[8], grads[9], grads[10], grads[11], grads[12], grads[13], grads[14], grads[15], grads[16], grads[17], grads[18], grads[19], grads[20], grads[21])
```

```python
import math
import types

import jax
import jax.numpy as jnp
from jax import lax
from jax.experimental import pallas as pl
from jax.experimental.pallas import tpu as pltpu
from jax.sharding import PartitionSpec as P

HEADS = 8
HEAD = 32
FOUR = 128

highest = lax.Precision.HIGHEST
f32 = jnp.float32
MESH = pl.DeviceIdType.MESH


def padded_2(x, sides, width):
    for axis, dim in sides:
        size, length = (lax.axis_size(axis), x.shape[dim])
        up = [(i, (i + 1) % size) for i in range(size - 1)]
        down = [(j, i) for i, j in up]
        last = lax.slice_in_dim(x, length - width, length, axis=dim)
        leading = lax.slice_in_dim(x, 0, width, axis=dim)
        before = lax.ppermute(last, axis, up)
        after = lax.ppermute(leading, axis, down)
        x = jnp.concatenate([before, x, after], axis=dim)
    return x


def matmul(left, right):
    return jnp.matmul(left, right, precision=highest)


def smooth(values):
    return jax.nn.gelu(values, approximate=True)


def layer_norm(values, norm_gain, norm_shift):
    average = jnp.mean(values, axis=-1, keepdims=True)
    center = values - average
    spread = jnp.mean(center * center, axis=-1, keepdims=True)
    return center * lax.rsqrt(spread + 1e-05) * norm_gain + norm_shift


def geometry(row_index, col_index, grid_sizes):
    size_rows = grid_sizes[:, 0]
    size_cols = grid_sizes[:, 1]
    within = (row_index[None, :, None] < size_rows[:, None, None]) & (
        col_index[None, None, :] < size_cols[:, None, None]
    )
    inside = within.astype(jnp.float32)
    coord_x = (row_index.astype(jnp.float32)[None, :, None] + 0.5) / size_rows.astype(jnp.float32)[
        :, None, None
    ] + 0.0 * inside
    coord_y = (col_index.astype(jnp.float32)[None, None, :] + 0.5) / size_cols.astype(jnp.float32)[
        :, None, None
    ] + 0.0 * inside
    points = (size_rows * size_cols).astype(jnp.float32)
    return (inside, coord_x, coord_y, points)


def features(coord_x, coord_y):
    angles = math.pi * (jnp.arange(FOUR // 4).astype(jnp.float32) + 1.0)
    along_x = coord_x[..., None] * angles
    along_y = coord_y[..., None] * angles
    return jnp.concatenate(
        [jnp.sin(along_x), jnp.cos(along_x), jnp.sin(along_y), jnp.cos(along_y)], axis=-1
    )


def rotate(vectors, coord_x, coord_y):
    quarter = HEAD // 4
    angles = 2.0 * math.pi * (jnp.arange(quarter).astype(jnp.float32) + 1.0)
    turn_x = coord_x[..., None, None] * angles
    turn_y = coord_y[..., None, None] * angles
    cosine_x, sine_x = (jnp.cos(turn_x), jnp.sin(turn_x))
    cosine_y, sine_y = (jnp.cos(turn_y), jnp.sin(turn_y))
    part_one = vectors[..., :quarter]
    part_two = vectors[..., quarter : 2 * quarter]
    part_three = vectors[..., 2 * quarter : 3 * quarter]
    part_four = vectors[..., 3 * quarter :]
    return jnp.concatenate(
        [
            part_one * cosine_x - part_two * sine_x,
            part_one * sine_x + part_two * cosine_x,
            part_three * cosine_y - part_four * sine_y,
            part_three * sine_y + part_four * cosine_y,
        ],
        axis=-1,
    )


def split_heads(values):
    return values.reshape(values.shape[:-1] + (HEADS, HEAD))


def conv_embed(padded, weight_in, bias_in):
    tile_rows = padded.shape[1] - 2
    tile_cols = padded.shape[2] - 2
    total = jnp.zeros(padded.shape[:1] + (tile_rows, tile_cols, weight_in.shape[-1]), jnp.float32)
    for shift_row in range(3):
        for shift_col in range(3):
            window = padded[
                :, shift_row : shift_row + tile_rows, shift_col : shift_col + tile_cols, :
            ]
            total = total + jnp.einsum(
                "brci,io->brco", window, weight_in[shift_row, shift_col], precision=highest
            )
    return total + bias_in


def conv_transpose(grad_padded, weight_in):
    tile_rows = grad_padded.shape[1] - 2
    tile_cols = grad_padded.shape[2] - 2
    total = jnp.zeros(
        grad_padded.shape[:1] + (tile_rows, tile_cols, weight_in.shape[2]), jnp.float32
    )
    for shift_row in range(3):
        for shift_col in range(3):
            window = grad_padded[
                :,
                2 - shift_row : 2 - shift_row + tile_rows,
                2 - shift_col : 2 - shift_col + tile_cols,
                :,
            ]
            total = total + jnp.einsum(
                "brco,io->brci", window, weight_in[shift_row, shift_col], precision=highest
            )
    return total


def project(params, hidden0, coord_x, coord_y):
    first_gain, first_shift, query_weight, key_weight, value_weight = params
    normed = layer_norm(hidden0, first_gain, first_shift)
    query_heads = rotate(split_heads(matmul(normed, query_weight)), coord_x, coord_y)
    key_heads = rotate(split_heads(matmul(normed, key_weight)), coord_x, coord_y)
    value_heads = split_heads(matmul(normed, value_weight))
    return (query_heads, key_heads, value_heads)


def summary(key_heads, value_heads, weight):
    return jnp.einsum(
        "brchd,brche->bhde", key_heads * weight[..., None, None], value_heads, precision=highest
    )


def encoder_rest(params, hidden0, query_heads, kv_summary):
    (
        output_weight,
        second_gain,
        second_shift,
        hidden_weight,
        hidden_bias,
        return_weight,
        return_bias,
    ) = params
    mixed = jnp.einsum("brchd,bhde->brche", query_heads, kv_summary, precision=highest).reshape(
        hidden0.shape
    )
    hidden1 = hidden0 + matmul(mixed, output_weight)
    normed = layer_norm(hidden1, second_gain, second_shift)
    return (
        hidden1
        + matmul(smooth(matmul(normed, hidden_weight) + hidden_bias), return_weight)
        + return_bias
    )


def decode_summary(params, hidden2, weight):
    decode_key, decode_value = params
    return summary(
        split_heads(matmul(hidden2, decode_key)), split_heads(matmul(hidden2, decode_value)), weight
    )


def decode_out(params, fourier, dec_summary, inside):
    decode_query, decode_output, propagate_up, propagate_bias, propagate_down, propagate_shift = (
        params
    )
    query_heads = split_heads(matmul(fourier, decode_query))
    mixed = jnp.einsum("brchd,bhde->brche", query_heads, dec_summary, precision=highest)
    latent = matmul(mixed.reshape(mixed.shape[:-2] + (HEADS * HEAD,)), decode_output)
    result = (
        latent
        + matmul(smooth(matmul(latent, propagate_up) + propagate_bias), propagate_down)
        + propagate_shift
    )
    return result * inside[..., None]


def general_body(
    field_in,
    conv_weight,
    conv_bias,
    first_gain,
    first_shift,
    query_weight,
    key_weight,
    value_weight,
    output_weight,
    second_gain,
    second_shift,
    hidden_weight,
    hidden_bias,
    return_weight,
    return_bias,
    decode_query,
    decode_key,
    decode_value,
    decode_output,
    propagate_up,
    propagate_bias,
    propagate_down,
    propagate_shift,
    cotangent,
    grid_sizes,
):
    both = ("row", "col")
    tile_rows = field_in.shape[1]
    tile_cols = field_in.shape[2]
    row_index = lax.axis_index("row") * tile_rows + jnp.arange(tile_rows, dtype=jnp.int32)
    col_index = lax.axis_index("col") * tile_cols + jnp.arange(tile_cols, dtype=jnp.int32)
    front_params = (first_gain, first_shift, query_weight, key_weight, value_weight)
    rest_params = (
        output_weight,
        second_gain,
        second_shift,
        hidden_weight,
        hidden_bias,
        return_weight,
        return_bias,
    )
    pair_params = (decode_key, decode_value)
    out_params = (
        decode_query,
        decode_output,
        propagate_up,
        propagate_bias,
        propagate_down,
        propagate_shift,
    )
    inside, coord_x, coord_y, points = geometry(row_index, col_index, grid_sizes)
    fourier = features(coord_x, coord_y)
    weight = inside / points[:, None, None]
    padded = padded_2(field_in * inside[..., None], (("row", 1), ("col", 2)), 1)
    hidden0 = conv_embed(padded, conv_weight, conv_bias)
    query_heads, key_heads, value_heads = project(front_params, hidden0, coord_x, coord_y)
    kv_summary = lax.psum(summary(key_heads, value_heads, weight), both)
    hidden2 = encoder_rest(rest_params, hidden0, query_heads, kv_summary)
    dec_summary = lax.psum(decode_summary(pair_params, hidden2, weight), both)

    def decode_local(params, summary_in):
        return decode_out(params, fourier, summary_in, inside)

    result, out_back = jax.vjp(decode_local, out_params, dec_summary)
    out_grads, dec_part = out_back(cotangent)
    dec_grad = lax.psum(dec_part, both)

    def pair_local(params, hidden_in):
        return decode_summary(params, hidden_in, weight)

    pair_grads, hidden2_grad = jax.vjp(pair_local, pair_params, hidden2)[1](dec_grad)
    rest_back = jax.vjp(encoder_rest, rest_params, hidden0, query_heads, kv_summary)[1]
    rest_grads, hidden0_part, query_grad, kv_part = rest_back(hidden2_grad)
    kv_grad = lax.psum(kv_part, both)

    def summary_local(key_in, value_in):
        return summary(key_in, value_in, weight)

    key_grad, value_grad = jax.vjp(summary_local, key_heads, value_heads)[1](kv_grad)

    def project_local(params, hidden_in):
        return project(params, hidden_in, coord_x, coord_y)

    front_grads, hidden0_more = jax.vjp(project_local, front_params, hidden0)[1](
        (query_grad, key_grad, value_grad)
    )
    hidden0_grad = hidden0_part + hidden0_more

    def conv_local(weight_in, bias_in):
        return conv_embed(padded, weight_in, bias_in)

    conv_grads = jax.vjp(conv_local, conv_weight, conv_bias)[1](hidden0_grad)
    grad_padded = padded_2(hidden0_grad, (("row", 1), ("col", 2)), 1)
    field_grad = conv_transpose(grad_padded, conv_weight) * inside[..., None]
    totals = lax.psum(
        (
            *conv_grads,
            *front_grads,
            *rest_grads,
            out_grads[0],
            *pair_grads,
            *out_grads[1:],
        ),
        both,
    )
    return (result, field_grad, *totals)


NT = 8
ITEMS = 16
ROWS, COLS = 4, 8
DEVICES = ROWS * COLS
PTS = 1024
D = 256

CHUNKS = ((0, 512, 1), (512, 512, 1), (1024, 512, 1), (1536, 512, 1), (2048, 512, 1), (2560, 512, 1), (3072, 512, 1), (3584, 256, 1), (3840, 256, 1))
R_UP, R_DOWN = 0, 512
R_DO, R_DQ, R_DK, R_DV = 1024, 1280, 1536, 1792
R_RET, R_HID, R_O, R_Q, R_V, R_K = 2048, 2560, 3072, 3328, 3584, 3840
G_ROWS = 4096
VECS = ("cb", "g1", "s1", "g2", "s2", "br", "ps", "bh", "bu")
SMALL = 8 * DEVICES
S_CONV, S_VEC = 0, 144
PLAN = ((), (), (0,), (1,), (), (), (), (), (), (), (2, 1), (), (), (), (), (0, 3), (), (), (4, 1), (5,), (3, 0), (), (2,), (), (1, 4), (), (6, 5), (2,), (0, 3, 1), (8,), (), (2, 4), (7, 5, 0, 4, 0, 8), ())
TAIL = (6, 1, 5, 2, 6, 7, 3, 8, 4, -1, 4, 6, 7, 8, 7, 3, 8, 8, -2, 5, 6, 3, 7, 6, 2, 5, 7)
AXES, PLANE, ALL = range(3)
SEMS = 32


def dot(a, b, ca, cb):
    return lax.dot_general(a, b, (((ca,), (cb,)), ((), ())), preferred_element_type=f32)


def cut(x):
    top = x.astype(jnp.bfloat16)
    return top, (x - top.astype(f32)).astype(jnp.bfloat16)


def dot3(a, b, ca, cb):
    (a0, a1), (b0, b1) = cut(a), cut(b)
    return dot(a0, b0, ca, cb) + (dot(a0, b1, ca, cb) + dot(a1, b0, ca, cb))


def nn(a, b):
    return dot3(a, b, 1, 0)


def nt(a, b):
    return dot3(a, b, 1, 1)


def tn(a, b):
    return dot3(a, b, 0, 0)


def dot_mark(e, b, ca):
    b0, b1 = cut(b)
    return dot(e, b0, ca, 0) + dot(e, b1, ca, 0)


def iota(shape, dim):
    return lax.broadcasted_iota(jnp.int32, shape, dim)


GC = math.sqrt(2.0 / math.pi)


def gelu_both(x):
    x2 = x * x
    t = jnp.tanh(GC * (x + 0.044715 * (x2 * x)))
    half = 0.5 * (1.0 + t)
    slope = half + 0.5 * x * (1.0 - t * t) * (GC + (3 * 0.044715 * GC) * x2)
    return x * half, slope


def turn_sin(u):
    return jnp.sin((2.0 * math.pi) * (u - jnp.round(u)))


def compact(z):
    lane = iota((HEAD, D), 1) // HEAD
    total = jnp.zeros((HEAD, D), f32)
    for h in range(HEADS):
        total = total + jnp.where(lane == h, z[h * HEAD : (h + 1) * HEAD, :], 0.0)
    return total


def expand(blocks):
    lane = iota((HEAD, D), 1) // HEAD
    return jnp.concatenate([jnp.where(lane == h, blocks, 0.0) for h in range(HEADS)], axis=0)


def swap_pairs(v):
    parts = []
    for s in range(D // 128):
        part = v[:, s * 128 : (s + 1) * 128]
        low = (iota(part.shape, 1) // 8) % 2 == 0
        parts.append(jnp.where(low, pltpu.roll(part, 120, 1), pltpu.roll(part, 8, 1)))
    return jnp.concatenate(parts, axis=1)


def norm_back(dn, nhat, rstd):
    a = jnp.mean(dn, axis=-1, keepdims=True)
    b = jnp.mean(dn * nhat, axis=-1, keepdims=True)
    return rstd * (dn - a - nhat * b)


def colsum(v):
    return jnp.sum(v, axis=0, keepdims=True)


def shift_cols(f, step):
    if step == 0:
        return f
    n = f.shape[1]
    lane = iota(f.shape, 1)
    col, tile = lane % 8, (lane // 64) % 8
    if step == 1:
        near, far = pltpu.roll(f, n - 1, 1), pltpu.roll(f, n - 57, 1)
        return jnp.where(col < 7, near, jnp.where(tile < COLS - 1, far, 0.0))
    near, far = pltpu.roll(f, 1, 1), pltpu.roll(f, 57, 1)
    return jnp.where(col > 0, near, jnp.where(tile > 0, far, 0.0))


def shift_rows(f, step):
    if step == 0:
        return f
    n = f.shape[1]
    lane = iota(f.shape, 1)
    row, tile = (lane // 8) % 8, lane // 512
    if step == 1:
        near, far = pltpu.roll(f, n - 8, 1), pltpu.roll(f, n - 456, 1)
        return jnp.where(row < 7, near, jnp.where(tile < ROWS - 1, far, 0.0))
    near, far = pltpu.roll(f, 8, 1), pltpu.roll(f, 456, 1)
    return jnp.where(row > 0, near, jnp.where(tile > 0, far, 0.0))


INPUTS = dict(
    fld=(NT * NT, 4, ITEMS),
    ct=(PTS, D),
    wc=(9, 4, D),
    cb=(1, D),
    g1=(1, D),
    s1=(1, D),
    wq=(D, D),
    wk=(D, D),
    wv=(D, D),
    wo=(D, D),
    g2=(1, D),
    s2=(1, D),
    wh=(D, 512),
    bh=(1, 512),
    wr=(512, D),
    br=(1, D),
    dq=(128, D),
    dk=(D, D),
    dv=(D, D),
    do=(D, D),
    wu=(D, 512),
    bu=(1, 512),
    wd=(512, D),
    ps=(1, D),
)


def kernel(*refs):
    gs, *refs = refs
    args, refs = refs[: len(INPUTS)], refs[len(INPUTS) :]
    o_res, o_fg, o_small, o_g, *refs = refs
    R = types.SimpleNamespace(**dict(zip([*SCRATCH, *INPUTS], refs, strict=True)))
    G = R.G
    row, col = lax.axis_index("row"), lax.axis_index("col")
    me = row * COLS + col
    core, xbit, ybit = col % 2, (col // 2) % 2, col // 4
    item = me // 2

    def at(number):
        return (number // COLS, number % COLS)

    def remote(src, dst, send, recv, to):
        copy = pltpu.make_async_remote_copy(
            src_ref=src, dst_ref=dst, send_sem=send, recv_sem=recv, device_id=to, device_id_type=MESH
        )
        copy.start()
        return copy

    def drain(ref, sem):
        pltpu.make_async_copy(ref, ref, sem).wait()

    def send_or_copy(src, dst, send, recv, number):
        @pl.when(number != me)
        def _():
            remote(src, dst, send, recv, at(number))

        @pl.when(number == me)
        def _():
            pltpu.make_async_copy(src, dst, recv).start()

    loads = {}
    for i, n in enumerate(INPUTS):
        loads[n] = pltpu.make_async_copy(args[i], getattr(R, n), R.s_in.at[i])
        loads[n].start()

    def need(*wanted):
        for n in wanted:
            loads.pop(n).wait()

    barrier = pltpu.get_barrier_semaphore()
    for k in range(1, DEVICES):
        pl.semaphore_signal(
            barrier, inc=1, device_id=at((me + k) % DEVICES), device_id_type=MESH
        )

    need("fld")
    for ch in range(4):
        R.FA[pl.ds(ch, ITEMS, stride=8), pl.ds(0, 64)] = jnp.transpose(R.fld[:, ch, :])
    size_r, size_c = gs[0, item], gs[1, item]
    fr, fc = size_r.astype(f32), size_c.astype(f32)

    def rotary_tables():
        shape = (80, 128)
        k, lane = iota(shape, 0), iota(shape, 1)
        is_x = k < 16
        coord = jnp.where(
            is_x,
            ((16 * core + k).astype(f32) + 0.5) / fr,
            ((k - 16).astype(f32) + 0.5) / fc,
        )
        freq = (lane % 8 + 1).astype(f32)
        quarter = (lane // 8) % 4
        keep = is_x == (quarter < 2)
        turns = freq * coord
        turns = turns - jnp.round(turns)
        cos_t = jnp.where(keep, turn_sin(turns + 0.25), 0.0)
        sin_t = jnp.where(keep, turn_sin(turns), 0.0)
        sin_t = jnp.where(quarter % 2 == 0, -sin_t, sin_t)
        p, t = iota((PTS, 80), 0), iota((PTS, 80), 1)
        pick = (t == 8 * (p // 512) + (p // 8) % 8) | (t - 16 == 8 * ((p // 64) % 8) + p % 8)
        R.rot[...] = dot_mark(
            pick.astype(jnp.bfloat16), jnp.concatenate([cos_t, sin_t], axis=1), 1
        )

    def fourier_tables():
        shape = (96, 128)
        k, lane = iota(shape, 0), iota(shape, 1)
        is_x = k < 32
        coord = jnp.where(is_x, (k.astype(f32) + 0.5) / fr, ((k - 32).astype(f32) + 0.5) / fc)
        turns = 0.5 * ((lane % 32 + 1).astype(f32) * coord)
        turns = turns - jnp.round(turns)
        turns = jnp.where((lane // 32) % 2 == 0, turns, turns + 0.25)
        R.FF[...] = jnp.where(is_x == (lane < 64), turn_sin(turns), 0.0)

    def tile_masks():
        p = iota((PTS, 128), 0)
        here_r = 16 * core + 8 * (p // 512) + (p // 8) % 8
        here_c = 8 * ((p // 64) % 8) + p % 8
        inv_points = 1.0 / (fr * fc)
        R.wgt[...] = jnp.where((here_r < size_r) & (here_c < size_c), inv_points, 0.0)
        for b in range(ITEMS):
            p = iota((64, 128), 0)
            ok = (NT * row + (p // 8) % 8 < gs[0, b]) & (NT * col + p % 8 < gs[1, b])
            R.mask[pl.ds(64 * b, 64)] = ok.astype(f32)
        p, t = iota((PTS, D), 0), iota((PTS, D), 1)
        chosen = (p // 64 == t // 16) & (
            ((t % 16) == (p // 8) % 8) | ((t % 16) == 8 + p % 8)
        )
        R.E[...] = chosen.astype(jnp.bfloat16)

    rotary_tables()
    fourier_tables()
    tile_masks()
    need("ct", "wd")
    mask2 = jnp.concatenate([R.mask[...]] * 2, axis=1)
    R.ctm[...] = R.ct[...] * mask2
    need("wc")
    R.W9[...] = jnp.zeros((72, D), f32)
    for k in range(9):
        R.W9[pl.ds(8 * k, 4)] = R.wc[k]
    pl.semaphore_wait(barrier, DEVICES - 1)

    for k in range(1, DEVICES):
        to = (me + k) % DEVICES
        remote(
            R.FA.at[pl.ds((to // 2) * 8, 4)],
            R.FR.at[pl.ds(me * 8, 4)],
            R.s_f.at[0],
            R.r_f.at[0],
            at(to),
        )
    R.FR[pl.ds(me * 8, 4)] = R.FA[pl.ds(item * 8, 4)]

    R.dact[...] = nt(R.ctm[...], R.wd[...])
    R.rcc[...] = dot_mark(R.E[...], R.ctm[...], 0)
    ps_grad = colsum(R.ctm[...])

    def cossin():
        c, s = R.rot[:, :128], R.rot[:, 128:]
        return jnp.concatenate([c, c], axis=1), jnp.concatenate([s, s], axis=1)

    def turn(v):
        c, s = cossin()
        return v * c + swap_pairs(v) * s

    def turn_back(v):
        c, s = cossin()
        return v * c - swap_pairs(v) * s

    def wgt2():
        return jnp.concatenate([R.wgt[...]] * 2, axis=1)

    need(*list(loads))
    drain(R.FR.at[pl.ds(0, 4 * (DEVICES - 1))], R.r_f.at[0])
    lane, sub = iota((8, DEVICES * 64), 1), iota((8, DEVICES * 64), 0)
    full_r, full_c = 8 * (lane // 512) + (lane // 8) % 8, 8 * ((lane // 64) % 8) + lane % 8
    full_mask = (full_r < size_r) & (full_c < size_c) & (sub < 4)
    low = iota((8, 128), 1) < 64
    pieces = []
    for k in range(DEVICES // 2):
        left = R.FR[pl.ds(16 * k, 8)]
        right = R.FR[pl.ds(16 * k + 8, 8)]
        pieces.append(jnp.where(low, left, pltpu.roll(right, 64, 1)))
    field = jnp.where(full_mask, jnp.concatenate(pieces, axis=1), 0.0)
    for dj in range(3):
        along = shift_cols(field, dj - 1)
        for di in range(3):
            patch = shift_rows(along, di - 1)
            mine = jnp.where(core == 0, patch[:, :PTS], patch[:, PTS:])
            R.PT[pl.ds((di * 3 + dj) * 8, 8)] = mine

    hidden0 = tn(R.PT[...], R.W9[...]) + R.cb[...]
    R.h0[...] = hidden0
    mean = jnp.mean(hidden0, axis=-1, keepdims=True)
    center = hidden0 - mean
    rstd1 = lax.rsqrt(jnp.mean(center * center, axis=-1, keepdims=True) + 1e-5)
    R.rs1[...] = jnp.broadcast_to(rstd1, (PTS, 128))
    R.n1[...] = center * rstd1
    R.n[...] = R.n1[...] * R.g1[...] + R.s1[...]
    R.k[...] = turn(nn(R.n[...], R.wk[...]))
    R.wn[...] = R.n[...] * wgt2()
    R.T[...] = tn(R.k[...], R.wn[...])

    pair = (row, col + 1 - 2 * core)

    def swap_start(i, value):
        R.XS[i] = value
        return remote(R.XS.at[i], R.XR.at[i], R.s_x.at[i], R.r_x.at[i], pair)

    def swap_end(i, copy):
        copy.wait()
        return R.XS[i] + R.XR[i]

    going = swap_start(0, compact(nn(R.T[...], R.wv[...])))
    R.q[...] = turn(nn(R.n[...], R.wq[...]))
    R.KV[...] = expand(swap_end(0, going))
    R.KVO[...] = nn(R.KV[...], R.wo[...])
    hidden1 = R.h0[...] + nn(R.q[...], R.KVO[...])
    mean = jnp.mean(hidden1, axis=-1, keepdims=True)
    center = hidden1 - mean
    rstd2 = lax.rsqrt(jnp.mean(center * center, axis=-1, keepdims=True) + 1e-5)
    R.rs2[...] = jnp.broadcast_to(rstd2, (PTS, 128))
    R.m1[...] = center * rstd2
    R.m[...] = R.m1[...] * R.g2[...] + R.s2[...]
    R.h1[...] = hidden1 + R.br[...]
    a, slope = gelu_both(nn(R.m[...], R.wh[...]) + R.bh[...])
    R.a[...] = a
    R.az[...] = slope
    R.h2[...] = R.h1[...] + nn(R.a[...], R.wr[...])
    R.gram[...] = tn(R.h2[...], R.h2[...] * wgt2())
    half = nn(tn(R.dk[...], R.gram[...]), R.dv[...])
    going = swap_start(1, compact(half))
    R.DS[...] = expand(swap_end(1, going))
    R.P1[...] = nn(R.dq[...], R.DS[...])
    R.AB[...] = nn(R.FF[...], nn(R.P1[...], R.do[...]))

    for k in range(16):
        R.TS[k, pl.ds(0, 8)] = R.AB[pl.ds(16 * core + 8 * (k // 8), 8)]
        R.TS[k, pl.ds(8, 8)] = R.AB[pl.ds(32 + 8 * (k % 8), 8)]
    for k in range(16):
        slot = (me + k) % 16
        send_or_copy(
            R.TS.at[slot],
            R.TR.at[item],
            R.s_t.at[0],
            R.r_t.at[item],
            16 * core + slot,
        )
    for b in range(ITEMS):
        drain(R.TR.at[b], R.r_t.at[b])

    first, second = (
        xbit * (1 - core) + ybit * core,
        ybit * (1 - core) + xbit * core,
    )
    step_x, step_y = 2 - 4 * xbit, 4 - 8 * ybit
    col_first = col + step_x * (1 - core) + step_y * core
    col_second = col + step_y * (1 - core) + step_x * core

    def sum_chunk(i):
        o, n, kind = CHUNKS[i]
        buf, used, free = R.RB, [SEMS * i], [o]
        place = 2 * ybit + xbit
        half_at = o + core * (n // 2)
        quarter_at = half_at + first * (n // 4)
        eighth_at = quarter_at + second * (n // 8) if kind == AXES else half_at + place * (n // 8)
        shard_at = eighth_at + row * (n // 32)
        plane = [
            (row, col + step_x, 2 * ybit + 1 - xbit),
            (row, col + step_y, 2 * (1 - ybit) + xbit),
            (row, col + step_x + step_y, 2 * (1 - ybit) + 1 - xbit),
        ]
        here = (row, col, place)
        line = [((row + z) % ROWS, col) for z in range(1, ROWS)]

        def part(ref, start, count):
            return ref.at[pl.ds(pl.multiple_of(start, 8), count)]

        def go(src, dst, to):
            copy = remote(src, dst, R.s_g.at[used[0]], R.r_g.at[used[0]], to)
            used[0] += 1
            return copy

        def give(mine, count, *away):
            copies, came = [], []
            for start, to in away:
                here = buf.at[pl.ds(free[0], count)]
                free[0] += count
                came.append(here)
                copies.append(go(part(G, start, count), here, to))

            def add(into):
                for copy in copies:
                    copy.wait()
                total = part(G, mine, count)[...]
                for here in came:
                    total = total + here[...]
                part(into, mine, count)[...] = total

            return add

        def spread(mine, count, *to):
            rows = part(R.SUM, mine, count)
            copies = [go(rows, rows, device) for device in to]

            def wait():
                for copy in copies:
                    copy.wait()

            return wait

        add = give(half_at, n // 2, (o + (1 - core) * (n // 2), pair))
        yield
        add(G)
        if kind == ALL:
            chips = [((row + z) % ROWS, c, p) for z in range(ROWS) for _, c, p in [here, *plane]][1:]
            away = [(half_at + (4 * p + r) * (n // 32), (r, c)) for r, c, p in chips]
            shard_at = half_at + (4 * place + row) * (n // 32)
            add = give(shard_at, n // 32, *away)
            yield
            add(R.SUM)
            wait = spread(shard_at, n // 32, *[(r, c) for r, c, _ in chips])
            yield
            wait()
        elif kind == PLANE:
            away = [(half_at + p * (n // 8), (r, c)) for r, c, p in plane]
            add = give(eighth_at, n // 8, *away)
            yield
            add(G)
        else:
            away = half_at + (1 - first) * (n // 4)
            add = give(quarter_at, n // 4, (away, (row, col_first)))
            yield
            add(G)
            away = quarter_at + (1 - second) * (n // 8)
            add = give(eighth_at, n // 8, (away, (row, col_second)))
            yield
            add(G)
        if kind != ALL:
            away = [(eighth_at + to[0] * (n // 32), to) for to in line]
            add = give(shard_at, n // 32, *away)
            yield
            add(R.SUM)
            wait = spread(shard_at, n // 32, *line)
            yield
            wait()
        if kind == PLANE:
            wait = spread(eighth_at, n // 8, *[(r, c) for r, c, _ in plane])
            yield
            wait()
        elif kind == AXES:
            wait = spread(eighth_at, n // 8, (row, col_second))
            yield
            wait()
            wait = spread(quarter_at, n // 4, (row, col_first))
            yield
            wait()
        wait = spread(half_at, n // 2, pair)
        yield
        wait()
        out = pltpu.make_async_copy(
            R.SUM.at[pl.ds(o, n)], o_g.at[pl.ds(o, n)], R.s_o.at[1 + i]
        )
        out.start()
        outs.append(out)

    going_on, outs, plan = {}, [], list(PLAN)

    def launch(*ready):
        for i, chunk in enumerate(CHUNKS):
            if chunk[0] in ready:
                going_on[i] = sum_chunk(i)
                next(going_on[i])
        step()

    def advance(i):
        if next(going_on[i], i) == i:
            del going_on[i]

    def step():
        for i in plan.pop(0):
            advance(i)

    table = R.TR[...].reshape(ITEMS * 16, D)
    R.UT[...] = nn(table, R.wu[...])
    a, slope = gelu_both(dot_mark(R.E[...], R.UT[...], 1) + R.bu[...])
    R.act[...] = a
    R.dpre[...] = slope * R.dact[...]
    R.rc[...] = dot_mark(R.E[...], R.dpre[...], 0)
    R.DAB[...] = (nt(R.rc[...], R.wu[...]) + R.rcc[...]).reshape(ITEMS, 16, D)
    for k in range(ITEMS):
        b = (item + k) % ITEMS
        send_or_copy(
            R.DAB.at[b],
            R.DR.at[me % 16],
            R.s_r.at[0],
            R.r_r.at[me % 16],
            2 * b + row // 2,
        )
    table = R.TR[...].reshape(ITEMS * 16, D)
    grad = tn(table, R.rc[...])
    G[pl.ds(R_UP, D)] = grad[:, :D]
    G[pl.ds(R_UP + D, D)] = grad[:, D:]
    launch(R_UP)
    G[pl.ds(R_DOWN, 512)] = tn(R.act[...], R.ctm[...])
    step()
    launch(R_DOWN)
    latent = dot_mark(R.E[...], table, 1)
    mask2 = jnp.concatenate([R.mask[...]] * 2, axis=1)
    R.res[...] = (latent + nn(R.act[...], R.wd[...]) + R.ps[...]) * mask2
    out_res = pltpu.make_async_copy(R.res, o_res, R.s_o.at[0])
    out_res.start()
    bu_grad = colsum(R.dpre[...])
    step()

    for k in range(16):
        drain(R.DR.at[k], R.r_r.at[k])
    step()
    da = [jnp.zeros((8, D), f32) for _ in range(2)]
    db = []
    for t in range(COLS):
        for s in range(2):
            da[s] = da[s] + R.DR[s * 8 + t, pl.ds(0, 8)]
        db.append(R.DR[t, pl.ds(8, 8)] + R.DR[8 + t, pl.ds(8, 8)])
    zero = jnp.zeros((8, D), f32)
    is0 = core == 0
    dab = jnp.concatenate(
        [
            jnp.where(is0, da[0], zero),
            jnp.where(is0, da[1], zero),
            jnp.where(is0, zero, da[0]),
            jnp.where(is0, zero, da[1]),
            *db,
        ],
        axis=0,
    )
    dm_table = tn(R.FF[...], dab)
    dp1 = nt(dm_table, R.do[...])
    going = swap_start(2, compact(tn(R.dq[...], dp1)))
    step()
    G[pl.ds(R_DO, D)] = tn(R.P1[...], dm_table)
    G[pl.ds(R_DQ, 128)] = nt(dp1, R.DS[...])
    G[pl.ds(R_DQ + 128, 128)] = jnp.zeros((128, D), f32)
    step()
    launch(R_DO)
    x2 = nn(R.gram[...], R.dv[...])
    step()
    dd = expand(swap_end(2, going))
    step()
    y1 = nn(R.dk[...], dd)
    dgram = nt(y1, R.dv[...]) + nt(R.dv[...], y1)
    step()
    R.dh[...] = nn(R.h2[...], dgram) * wgt2()
    step()
    G[pl.ds(R_DK, D)] = nt(x2, dd)
    G[pl.ds(R_DV, D)] = tn(R.gram[...], y1)
    step()
    launch(R_DK)
    br_grad = colsum(R.dh[...])
    G[pl.ds(R_RET, 512)] = tn(R.a[...], R.dh[...])
    step()
    launch(R_RET)
    R.dz[...] = nt(R.dh[...], R.wr[...]) * R.az[...]
    bh_grad = colsum(R.dz[...])
    step()
    grad = tn(R.m[...], R.dz[...])
    G[pl.ds(R_HID, D)] = grad[:, :D]
    G[pl.ds(R_HID + D, D)] = grad[:, D:]
    step()
    launch(R_HID)
    dm = nt(R.dz[...], R.wh[...])
    step()
    g2_grad, s2_grad = colsum(dm * R.m1[...]), colsum(dm)
    rs2 = jnp.concatenate([R.rs2[...]] * 2, axis=1)
    R.dh[...] = R.dh[...] + norm_back(dm * R.g2[...], R.m1[...], rs2)
    step()
    stat = tn(R.q[...], R.dh[...])
    going = swap_start(3, compact(nt(stat, R.wo[...])))
    step()
    G[pl.ds(R_O, D)] = tn(R.KV[...], stat)
    R.dq0[...] = turn_back(nt(R.dh[...], R.KVO[...]))
    step()
    G[pl.ds(R_Q, D)] = tn(R.n[...], R.dq0[...])
    step()
    launch(R_O, R_Q)
    dkv = expand(swap_end(3, going))
    G[pl.ds(R_V, D)] = tn(R.T[...], dkv)
    step()
    launch(R_V)
    dt = nt(dkv, R.wv[...])
    R.dk0[...] = turn_back(nt(R.wn[...], dt))
    step()
    G[pl.ds(R_K, D)] = tn(R.n[...], R.dk0[...])
    step()
    launch(R_K)
    dn = (
        nn(R.k[...], dt) * wgt2()
        + nt(R.dq0[...], R.wq[...])
        + nt(R.dk0[...], R.wk[...])
    )
    step()
    g1_grad, s1_grad = colsum(dn * R.n1[...]), colsum(dn)
    rs1 = jnp.concatenate([R.rs1[...]] * 2, axis=1)
    R.dh[...] = R.dh[...] + norm_back(dn * R.g1[...], R.n1[...], rs1)
    step()

    cb_grad = colsum(R.dh[...])
    conv_grad = nn(R.PT[...], R.dh[...])
    small = [conv_grad[:, :128], conv_grad[:, 128:]]
    vectors = [cb_grad, g1_grad, s1_grad, g2_grad, s2_grad, br_grad, ps_grad, bh_grad, bu_grad]
    for v in vectors:
        small += [v[:, 128 * k : 128 * (k + 1)] for k in range(v.shape[1] // 128)]
    small.append(jnp.zeros((SMALL - sum(v.shape[0] for v in small), 128), f32))
    small = jnp.concatenate(small, axis=0)
    dpt = nt(R.W9[...], R.dh[...])
    half_lane = iota((8, 2 * PTS), 1) // PTS == core
    back = jnp.zeros((8, 2 * PTS), f32)
    for di in range(3):
        line = jnp.zeros((8, 2 * PTS), f32)
        for dj in range(3):
            part = dpt[(di * 3 + dj) * 8 : (di * 3 + dj) * 8 + 8]
            part = jnp.where(half_lane, jnp.concatenate([part, part], axis=1), 0.0)
            line = line + shift_cols(part, 1 - dj)
        back = back + shift_rows(line, 1 - di)
    back = jnp.where(full_mask, back, 0.0)
    for k in range(DEVICES):
        R.FS[pl.ds(16 * k, 8)] = small[8 * k : 8 * k + 8]
        R.FS[pl.ds(16 * k + 8, 8)] = back[:, 128 * (k // 2) : 128 * (k // 2 + 1)]
    step()
    for k in range(1, DEVICES):
        to = (me + k) % DEVICES
        remote(
            R.FS.at[pl.ds(to * 16, 12)],
            R.FB.at[pl.ds(me * 16, 12)],
            R.s_b.at[0],
            R.r_b.at[0],
            at(to),
        )
    R.FB[pl.ds(me * 16, 12)] = R.FS[pl.ds(me * 16, 12)]
    step()

    def small_sums():
        drain(R.FB.at[pl.ds(0, 12 * (DEVICES - 1))], R.r_b.at[0])
        total = jnp.zeros((8, 128), f32)
        for k in range(DEVICES):
            total = total + R.FB[pl.ds(16 * k, 8)]
        mine = R.SS.at[pl.ds(me * 8, 8)]
        mine[...] = total
        for k in range(1, DEVICES):
            remote(mine, mine, R.s_s.at[0], R.r_s.at[0], at((me + k) % DEVICES))
        for b in range(ITEMS):
            both = R.FB[pl.ds(32 * b + 8, 8)] + R.FB[pl.ds(32 * b + 24, 8)]
            R.FO[pl.ds(8 * b, 8)] = jnp.where(core == 0, both, pltpu.roll(both, 64, 1))
        out = pltpu.make_async_copy(R.FO, o_fg, R.s_o.at[len(CHUNKS) + 1])
        out.start()
        outs.append(out)

    def small_end():
        drain(R.SS.at[pl.ds(0, 8 * (DEVICES - 1))], R.r_s.at[0])
        out = pltpu.make_async_copy(R.SS, o_small, R.s_o.at[len(CHUNKS) + 2])
        out.start()
        outs.append(out)

    for i in TAIL:
        if i == -1:
            small_sums()
        elif i == -2:
            small_end()
        else:
            advance(i)
    assert not going_on and not plan

    drain(R.FR.at[pl.ds(0, 4 * (DEVICES - 1))], R.s_f.at[0])
    drain(R.FB.at[pl.ds(0, 12 * (DEVICES - 1))], R.s_b.at[0])
    drain(R.SS.at[pl.ds(0, 8 * (DEVICES - 1))], R.s_s.at[0])
    inside_t = core == row // 2

    @pl.when(inside_t)
    def _():
        drain(R.TS.at[pl.ds(0, 15)], R.s_t.at[0])
        drain(R.DAB.at[pl.ds(0, 15)], R.s_r.at[0])

    @pl.when(jnp.logical_not(inside_t))
    def _():
        drain(R.TS, R.s_t.at[0])
        drain(R.DAB, R.s_r.at[0])

    out_res.wait()
    for out in outs:
        out.wait()


def vmem(*shape):
    return pltpu.VMEM(shape, f32)


SCRATCH = dict(
    G=vmem(G_ROWS, D),
    RB=vmem(G_ROWS, D),
    SUM=vmem(G_ROWS, D),
    FA=vmem(ITEMS * 8, 128),
    FR=vmem(DEVICES * 8, 128),
    FS=vmem(DEVICES * 16, 128),
    FB=vmem(DEVICES * 16, 128),
    FO=vmem(ITEMS * 8, 128),
    SS=vmem(SMALL, 128),
    W9=vmem(72, D),
    XS=vmem(4, HEAD, D),
    XR=vmem(4, HEAD, D),
    TS=vmem(16, 16, D),
    TR=vmem(ITEMS, 16, D),
    DAB=vmem(ITEMS, 16, D),
    DR=vmem(16, 16, D),
    mask=vmem(PTS, 128),
    wgt=vmem(PTS, 128),
    ctm=vmem(PTS, D),
    E=pltpu.VMEM((PTS, D), jnp.bfloat16),
    dact=vmem(PTS, 512),
    rcc=vmem(256, D),
    rc=vmem(256, 512),
    rot=vmem(PTS, D),
    FF=vmem(96, 128),
    PT=vmem(72, PTS),
    h0=vmem(PTS, D),
    rs1=vmem(PTS, 128),
    n1=vmem(PTS, D),
    n=vmem(PTS, D),
    wn=vmem(PTS, D),
    q=vmem(PTS, D),
    k=vmem(PTS, D),
    T=vmem(D, D),
    KV=vmem(D, D),
    KVO=vmem(D, D),
    rs2=vmem(PTS, 128),
    m1=vmem(PTS, D),
    m=vmem(PTS, D),
    h1=vmem(PTS, D),
    a=vmem(PTS, 512),
    az=vmem(PTS, 512),
    h2=vmem(PTS, D),
    gram=vmem(D, D),
    DS=vmem(D, D),
    P1=vmem(128, D),
    AB=vmem(96, D),
    UT=vmem(256, 512),
    act=vmem(PTS, 512),
    dpre=vmem(PTS, 512),
    res=vmem(PTS, D),
    dh=vmem(PTS, D),
    dz=vmem(PTS, 512),
    dq0=vmem(PTS, D),
    dk0=vmem(PTS, D),
    s_in=pltpu.SemaphoreType.DMA((len(INPUTS),)),
    s_f=pltpu.SemaphoreType.DMA((1,)),
    r_f=pltpu.SemaphoreType.DMA((1,)),
    s_b=pltpu.SemaphoreType.DMA((1,)),
    r_b=pltpu.SemaphoreType.DMA((1,)),
    s_t=pltpu.SemaphoreType.DMA((1,)),
    r_t=pltpu.SemaphoreType.DMA((16,)),
    s_r=pltpu.SemaphoreType.DMA((1,)),
    r_r=pltpu.SemaphoreType.DMA((16,)),
    s_x=pltpu.SemaphoreType.DMA((4,)),
    r_x=pltpu.SemaphoreType.DMA((4,)),
    s_s=pltpu.SemaphoreType.DMA((1,)),
    r_s=pltpu.SemaphoreType.DMA((1,)),
    s_g=pltpu.SemaphoreType.DMA((SEMS * len(CHUNKS),)),
    r_g=pltpu.SemaphoreType.DMA((SEMS * len(CHUNKS),)),
    s_o=pltpu.SemaphoreType.DMA((3 + len(CHUNKS),)),
)

PARTS = dict(
    wc=(9, 4, D),
    cb=(1, D),
    g1=(1, D),
    s1=(1, D),
    wq=(D, D),
    wk=(D, D),
    wv=(D, D),
    wo=(D, D),
    g2=(1, D),
    s2=(1, D),
    wh=(D, 512),
    bh=(1, 512),
    wr=(512, D),
    br=(1, D),
    dq=(128, D),
    dk=(D, D),
    dv=(D, D),
    do=(D, D),
    wu=(D, 512),
    bu=(1, 512),
    wd=(512, D),
    ps=(1, D),
)
ROW_AT = dict(
    wq=R_Q, wk=R_K, wv=R_V, wo=R_O, wr=R_RET, dq=R_DQ, dk=R_DK, dv=R_DV, do=R_DO, wd=R_DOWN,
    wh=R_HID, wu=R_UP,
)


SMALL_PARTS = tuple(name for name in PARTS if name not in ROW_AT)


def unpack(res_in, fg_in, small_in, g_in, res_out, fg_out, *rest):
    outs = dict(zip(PARTS, rest[: len(PARTS)], strict=True))
    res, fg, small, g, sem_in, sem_out, fg_here, *here = rest[len(PARTS) :]
    staged = dict(zip(SMALL_PARTS, here, strict=True))
    moves = []

    def add(src, here, *out):
        load = pltpu.make_async_copy(src, here, sem_in.at[len(moves)])
        load.start()
        moves.append((load, out))

    add(small_in, small)
    add(fg_in, fg)
    for k in range(4):
        part = pl.ds(k * 256, 256)
        add(res_in.at[part], res.at[part], (res.at[part], res_out.at[part]))
    for name, start in ROW_AT.items():
        count = 512 if name in ("wh", "wu") else PARTS[name][0]
        here = g.at[pl.ds(start, count)]
        if name in ("wh", "wu"):
            out = [
                (g.at[pl.ds(start + s * D, D)], outs[name].at[:, pl.ds(s * D, D)])
                for s in range(2)
            ]
        else:
            out = [(here, outs[name])]
        add(g_in.at[pl.ds(start, count)], here, *out)
    stores = []

    def store(src, dst):
        stores.append(pltpu.make_async_copy(src, dst, sem_out.at[len(stores)]))
        stores[-1].start()

    moves[0][0].wait()
    for k in range(9):
        staged["wc"][k, :, :128] = small[S_CONV + 8 * k : S_CONV + 8 * k + 4]
        staged["wc"][k, :, 128:] = small[S_CONV + 72 + 8 * k : S_CONV + 72 + 8 * k + 4]
    line = S_VEC
    for name in VECS:
        for k in range(PARTS[name][1] // 128):
            staged[name][:, 128 * k : 128 * (k + 1)] = small[line : line + 1]
            line += 1
    for name in SMALL_PARTS:
        store(staged[name], outs[name])
    moves[1][0].wait()
    for ch in range(4):
        fg_here[:, ch, :] = jnp.transpose(fg[pl.ds(ch, ITEMS, stride=8), pl.ds(0, 64)])
    store(fg_here, fg_out)
    for load, out in moves[2:]:
        load.wait()
        for src, dst in out:
            store(src, dst)
    for out in stores:
        out.wait()


ARGUMENTS = tuple(n for n in INPUTS if n not in ("fld", "ct"))


def item_body(field_in, *rest):
    values = dict(zip(ARGUMENTS + ("ct", "gs"), rest, strict=True))
    values["fld"] = field_in.transpose(1, 2, 3, 0)
    operands = [values["gs"].T]
    operands += [values[name].reshape(shape) for name, shape in INPUTS.items()]
    in_smem = pl.BlockSpec(memory_space=pltpu.SMEM)
    anywhere = pl.BlockSpec(memory_space=pl.ANY)
    made = pl.pallas_call(
        kernel,
        out_shape=(
            jax.ShapeDtypeStruct((PTS, D), f32),
            jax.ShapeDtypeStruct((ITEMS * 8, 128), f32),
            jax.ShapeDtypeStruct((SMALL, 128), f32),
            jax.ShapeDtypeStruct((G_ROWS, D), f32),
        ),
        in_specs=[in_smem] + [anywhere] * len(INPUTS),
        out_specs=(anywhere,) * 4,
        scratch_shapes=[*SCRATCH.values()] + [vmem(*shape) for shape in INPUTS.values()],
        compiler_params=pltpu.CompilerParams(
            collective_id=1, has_side_effects=True, vmem_limit_bytes=60 * 2**20
        ),
        name="layer",
    )(*operands)
    outs = pl.pallas_call(
        unpack,
        out_shape=(
            jax.ShapeDtypeStruct((PTS, D), f32),
            jax.ShapeDtypeStruct((NT * NT, 4, ITEMS), f32),
            *(jax.ShapeDtypeStruct(shape, f32) for shape in PARTS.values()),
        ),
        in_specs=[anywhere] * 4,
        out_specs=(anywhere,) * (2 + len(PARTS)),
        scratch_shapes=[
            vmem(PTS, D),
            vmem(ITEMS * 8, 128),
            vmem(SMALL, 128),
            vmem(G_ROWS, D),
            pltpu.SemaphoreType.DMA((24,)),
            pltpu.SemaphoreType.DMA((40,)),
            vmem(NT * NT, 4, ITEMS),
            *(vmem(*PARTS[name]) for name in SMALL_PARTS),
        ],
        compiler_params=pltpu.CompilerParams(vmem_limit_bytes=60 * 2**20),
        name="unpack",
    )(*made)
    shaped = []
    for name, value in zip(PARTS, outs[2:], strict=True):
        if name == "wc":
            value = value.reshape(3, 3, 4, D)
        elif name in VECS:
            value = value.reshape(-1)
        shaped.append(value)
    return (
        outs[0].reshape(ITEMS, NT, NT, D),
        outs[1].reshape(NT, NT, 4, ITEMS).transpose(3, 0, 1, 2),
        *shaped,
    )


def body(field_in, *rest):
    tile = field_in.shape[:3]
    mesh = (lax.axis_size("row"), lax.axis_size("col"))
    if mesh == (ROWS, COLS) and tile == (ITEMS, NT, NT):
        return item_body(field_in, *rest)
    return general_body(field_in, *rest)


def solution(mesh):
    spread = P(None, "row", "col", None)
    placed = (spread,) + (P(),) * 22 + (spread, P())
    return jax.shard_map(
        body,
        mesh=mesh,
        in_specs=placed,
        out_specs=(spread, spread) + (P(),) * 22,
        check_vma=False,
    )
```

```python
import math
import types

import jax
import jax.numpy as jnp
from jax import lax
from jax.experimental import pallas as pl
from jax.experimental.pallas import tpu as pltpu
from jax.sharding import PartitionSpec as P

HEADS = 8
HEAD = 32
FOUR = 128

highest = lax.Precision.HIGHEST
f32 = jnp.float32
MESH = pl.DeviceIdType.MESH


def padded_2(x, sides, width):
    for axis, dim in sides:
        size, length = (lax.axis_size(axis), x.shape[dim])
        up = [(i, (i + 1) % size) for i in range(size - 1)]
        down = [(j, i) for i, j in up]
        last = lax.slice_in_dim(x, length - width, length, axis=dim)
        leading = lax.slice_in_dim(x, 0, width, axis=dim)
        before = lax.ppermute(last, axis, up)
        after = lax.ppermute(leading, axis, down)
        x = jnp.concatenate([before, x, after], axis=dim)
    return x


def matmul(left, right):
    return jnp.matmul(left, right, precision=highest)


def smooth(values):
    return jax.nn.gelu(values, approximate=True)


def layer_norm(values, norm_gain, norm_shift):
    average = jnp.mean(values, axis=-1, keepdims=True)
    center = values - average
    spread = jnp.mean(center * center, axis=-1, keepdims=True)
    return center * lax.rsqrt(spread + 1e-05) * norm_gain + norm_shift


def geometry(row_index, col_index, grid_sizes):
    size_rows = grid_sizes[:, 0]
    size_cols = grid_sizes[:, 1]
    within = (row_index[None, :, None] < size_rows[:, None, None]) & (
        col_index[None, None, :] < size_cols[:, None, None]
    )
    inside = within.astype(jnp.float32)
    coord_x = (row_index.astype(jnp.float32)[None, :, None] + 0.5) / size_rows.astype(jnp.float32)[
        :, None, None
    ] + 0.0 * inside
    coord_y = (col_index.astype(jnp.float32)[None, None, :] + 0.5) / size_cols.astype(jnp.float32)[
        :, None, None
    ] + 0.0 * inside
    points = (size_rows * size_cols).astype(jnp.float32)
    return (inside, coord_x, coord_y, points)


def features(coord_x, coord_y):
    angles = math.pi * (jnp.arange(FOUR // 4).astype(jnp.float32) + 1.0)
    along_x = coord_x[..., None] * angles
    along_y = coord_y[..., None] * angles
    return jnp.concatenate(
        [jnp.sin(along_x), jnp.cos(along_x), jnp.sin(along_y), jnp.cos(along_y)], axis=-1
    )


def rotate(vectors, coord_x, coord_y):
    quarter = HEAD // 4
    angles = 2.0 * math.pi * (jnp.arange(quarter).astype(jnp.float32) + 1.0)
    turn_x = coord_x[..., None, None] * angles
    turn_y = coord_y[..., None, None] * angles
    cosine_x, sine_x = (jnp.cos(turn_x), jnp.sin(turn_x))
    cosine_y, sine_y = (jnp.cos(turn_y), jnp.sin(turn_y))
    part_one = vectors[..., :quarter]
    part_two = vectors[..., quarter : 2 * quarter]
    part_three = vectors[..., 2 * quarter : 3 * quarter]
    part_four = vectors[..., 3 * quarter :]
    return jnp.concatenate(
        [
            part_one * cosine_x - part_two * sine_x,
            part_one * sine_x + part_two * cosine_x,
            part_three * cosine_y - part_four * sine_y,
            part_three * sine_y + part_four * cosine_y,
        ],
        axis=-1,
    )


def split_heads(values):
    return values.reshape(values.shape[:-1] + (HEADS, HEAD))


def conv_embed(padded, weight_in, bias_in):
    tile_rows = padded.shape[1] - 2
    tile_cols = padded.shape[2] - 2
    total = jnp.zeros(padded.shape[:1] + (tile_rows, tile_cols, weight_in.shape[-1]), jnp.float32)
    for shift_row in range(3):
        for shift_col in range(3):
            window = padded[
                :, shift_row : shift_row + tile_rows, shift_col : shift_col + tile_cols, :
            ]
            total = total + jnp.einsum(
                "brci,io->brco", window, weight_in[shift_row, shift_col], precision=highest
            )
    return total + bias_in


def conv_transpose(grad_padded, weight_in):
    tile_rows = grad_padded.shape[1] - 2
    tile_cols = grad_padded.shape[2] - 2
    total = jnp.zeros(
        grad_padded.shape[:1] + (tile_rows, tile_cols, weight_in.shape[2]), jnp.float32
    )
    for shift_row in range(3):
        for shift_col in range(3):
            window = grad_padded[
                :,
                2 - shift_row : 2 - shift_row + tile_rows,
                2 - shift_col : 2 - shift_col + tile_cols,
                :,
            ]
            total = total + jnp.einsum(
                "brco,io->brci", window, weight_in[shift_row, shift_col], precision=highest
            )
    return total


def project(params, hidden0, coord_x, coord_y):
    first_gain, first_shift, query_weight, key_weight, value_weight = params
    normed = layer_norm(hidden0, first_gain, first_shift)
    query_heads = rotate(split_heads(matmul(normed, query_weight)), coord_x, coord_y)
    key_heads = rotate(split_heads(matmul(normed, key_weight)), coord_x, coord_y)
    value_heads = split_heads(matmul(normed, value_weight))
    return (query_heads, key_heads, value_heads)


def summary(key_heads, value_heads, weight):
    return jnp.einsum(
        "brchd,brche->bhde", key_heads * weight[..., None, None], value_heads, precision=highest
    )


def encoder_rest(params, hidden0, query_heads, kv_summary):
    (
        output_weight,
        second_gain,
        second_shift,
        hidden_weight,
        hidden_bias,
        return_weight,
        return_bias,
    ) = params
    mixed = jnp.einsum("brchd,bhde->brche", query_heads, kv_summary, precision=highest).reshape(
        hidden0.shape
    )
    hidden1 = hidden0 + matmul(mixed, output_weight)
    normed = layer_norm(hidden1, second_gain, second_shift)
    return (
        hidden1
        + matmul(smooth(matmul(normed, hidden_weight) + hidden_bias), return_weight)
        + return_bias
    )


def decode_summary(params, hidden2, weight):
    decode_key, decode_value = params
    return summary(
        split_heads(matmul(hidden2, decode_key)), split_heads(matmul(hidden2, decode_value)), weight
    )


def decode_out(params, fourier, dec_summary, inside):
    decode_query, decode_output, propagate_up, propagate_bias, propagate_down, propagate_shift = (
        params
    )
    query_heads = split_heads(matmul(fourier, decode_query))
    mixed = jnp.einsum("brchd,bhde->brche", query_heads, dec_summary, precision=highest)
    latent = matmul(mixed.reshape(mixed.shape[:-2] + (HEADS * HEAD,)), decode_output)
    result = (
        latent
        + matmul(smooth(matmul(latent, propagate_up) + propagate_bias), propagate_down)
        + propagate_shift
    )
    return result * inside[..., None]


def general_body(
    field_in,
    conv_weight,
    conv_bias,
    first_gain,
    first_shift,
    query_weight,
    key_weight,
    value_weight,
    output_weight,
    second_gain,
    second_shift,
    hidden_weight,
    hidden_bias,
    return_weight,
    return_bias,
    decode_query,
    decode_key,
    decode_value,
    decode_output,
    propagate_up,
    propagate_bias,
    propagate_down,
    propagate_shift,
    cotangent,
    grid_sizes,
):
    both = ("row", "col")
    tile_rows = field_in.shape[1]
    tile_cols = field_in.shape[2]
    row_index = lax.axis_index("row") * tile_rows + jnp.arange(tile_rows, dtype=jnp.int32)
    col_index = lax.axis_index("col") * tile_cols + jnp.arange(tile_cols, dtype=jnp.int32)
    front_params = (first_gain, first_shift, query_weight, key_weight, value_weight)
    rest_params = (
        output_weight,
        second_gain,
        second_shift,
        hidden_weight,
        hidden_bias,
        return_weight,
        return_bias,
    )
    pair_params = (decode_key, decode_value)
    out_params = (
        decode_query,
        decode_output,
        propagate_up,
        propagate_bias,
        propagate_down,
        propagate_shift,
    )
    inside, coord_x, coord_y, points = geometry(row_index, col_index, grid_sizes)
    fourier = features(coord_x, coord_y)
    weight = inside / points[:, None, None]
    padded = padded_2(field_in * inside[..., None], (("row", 1), ("col", 2)), 1)
    hidden0 = conv_embed(padded, conv_weight, conv_bias)
    query_heads, key_heads, value_heads = project(front_params, hidden0, coord_x, coord_y)
    kv_summary = lax.psum(summary(key_heads, value_heads, weight), both)
    hidden2 = encoder_rest(rest_params, hidden0, query_heads, kv_summary)
    dec_summary = lax.psum(decode_summary(pair_params, hidden2, weight), both)

    def decode_local(params, summary_in):
        return decode_out(params, fourier, summary_in, inside)

    result, out_back = jax.vjp(decode_local, out_params, dec_summary)
    out_grads, dec_part = out_back(cotangent)
    dec_grad = lax.psum(dec_part, both)

    def pair_local(params, hidden_in):
        return decode_summary(params, hidden_in, weight)

    pair_grads, hidden2_grad = jax.vjp(pair_local, pair_params, hidden2)[1](dec_grad)
    rest_back = jax.vjp(encoder_rest, rest_params, hidden0, query_heads, kv_summary)[1]
    rest_grads, hidden0_part, query_grad, kv_part = rest_back(hidden2_grad)
    kv_grad = lax.psum(kv_part, both)

    def summary_local(key_in, value_in):
        return summary(key_in, value_in, weight)

    key_grad, value_grad = jax.vjp(summary_local, key_heads, value_heads)[1](kv_grad)

    def project_local(params, hidden_in):
        return project(params, hidden_in, coord_x, coord_y)

    front_grads, hidden0_more = jax.vjp(project_local, front_params, hidden0)[1](
        (query_grad, key_grad, value_grad)
    )
    hidden0_grad = hidden0_part + hidden0_more

    def conv_local(weight_in, bias_in):
        return conv_embed(padded, weight_in, bias_in)

    conv_grads = jax.vjp(conv_local, conv_weight, conv_bias)[1](hidden0_grad)
    grad_padded = padded_2(hidden0_grad, (("row", 1), ("col", 2)), 1)
    field_grad = conv_transpose(grad_padded, conv_weight) * inside[..., None]
    totals = lax.psum(
        (
            *conv_grads,
            *front_grads,
            *rest_grads,
            out_grads[0],
            *pair_grads,
            *out_grads[1:],
        ),
        both,
    )
    return (result, field_grad, *totals)


NT = 8
ITEMS = 16
ROWS, COLS = 4, 8
DEVICES = ROWS * COLS
PTS = 1024
D = 256

CHUNKS = ((0, 512, 0), (512, 512, 0), (1024, 768, 0), (1792, 512, 0), (2304, 512, 0), (2816, 512, 1), (3328, 256, 1), (3584, 256, 1), (3840, 256, 1))
R_UP, R_DOWN = 0, 512
R_DO, R_DK, R_DV = 1024, 1280, 1536
R_RET, R_HID, R_O, R_Q, R_V, R_K = 1792, 2304, 2816, 3072, 3328, 3584
R_DQ, R_SMALL = 3840, 3968
G_ROWS = 4096
VECS = ("cb", "g1", "s1", "g2", "s2", "br", "ps", "bh", "bu")
S_CONV, S_VEC = 0, 72
PLAN = ((), (0,), (1,), (0, 1), (), (), (), (), (), (), (), (), (), (0,), (), (), (2, 1), (), (), (3, 0), (4,), (2,), (), (), (), (), (3, 1, 0), (2,), (4,), (5, 3), (1, 4, 6, 7), (3,), (0, 4, 2, 1, 6, 7, 8, 3, 0, 5), ())
TAIL = (4, 3, 7, 2, 6, 4, 8, 5, 7, -1, 2, 4, 6, 8, 3, 1, 7, 5, 2, 4, 8, 2, 3, 5, 0, 6, 8, 5, 1, 7, 6, 8)
AXES, PLANE, ALL = range(3)
SEMS = 32


def dot(a, b, ca, cb):
    return lax.dot_general(a, b, (((ca,), (cb,)), ((), ())), preferred_element_type=f32)


def cut(x):
    top = x.astype(jnp.bfloat16)
    return top, (x - top.astype(f32)).astype(jnp.bfloat16)


def dot3(a, b, ca, cb):
    (a0, a1), (b0, b1) = cut(a), cut(b)
    return dot(a0, b0, ca, cb) + (dot(a0, b1, ca, cb) + dot(a1, b0, ca, cb))


def nn(a, b):
    return dot3(a, b, 1, 0)


def nt(a, b):
    return dot3(a, b, 1, 1)


def tn(a, b):
    return dot3(a, b, 0, 0)


def dot_mark(e, b, ca):
    b0, b1 = cut(b)
    return dot(e, b0, ca, 0) + dot(e, b1, ca, 0)


def iota(shape, dim):
    return lax.broadcasted_iota(jnp.int32, shape, dim)


GC = math.sqrt(2.0 / math.pi)


def gelu_both(x):
    x2 = x * x
    t = jnp.tanh(GC * (x + 0.044715 * (x2 * x)))
    half = 0.5 * (1.0 + t)
    slope = half + 0.5 * x * (1.0 - t * t) * (GC + (3 * 0.044715 * GC) * x2)
    return x * half, slope


def turn_sin(u):
    return jnp.sin((2.0 * math.pi) * (u - jnp.round(u)))


def compact(z):
    lane = iota((HEAD, D), 1) // HEAD
    total = jnp.zeros((HEAD, D), f32)
    for h in range(HEADS):
        total = total + jnp.where(lane == h, z[h * HEAD : (h + 1) * HEAD, :], 0.0)
    return total


def expand(blocks):
    lane = iota((HEAD, D), 1) // HEAD
    return jnp.concatenate([jnp.where(lane == h, blocks, 0.0) for h in range(HEADS)], axis=0)


def swap_pairs(v):
    parts = []
    for s in range(D // 128):
        part = v[:, s * 128 : (s + 1) * 128]
        low = (iota(part.shape, 1) // 8) % 2 == 0
        parts.append(jnp.where(low, pltpu.roll(part, 120, 1), pltpu.roll(part, 8, 1)))
    return jnp.concatenate(parts, axis=1)


def norm_back(dn, nhat, rstd):
    a = jnp.mean(dn, axis=-1, keepdims=True)
    b = jnp.mean(dn * nhat, axis=-1, keepdims=True)
    return rstd * (dn - a - nhat * b)


def colsum(v):
    return jnp.sum(v, axis=0, keepdims=True)


def shift_cols(f, step):
    if step == 0:
        return f
    n = f.shape[1]
    lane = iota(f.shape, 1)
    col, tile = lane % 8, (lane // 64) % 8
    if step == 1:
        near, far = pltpu.roll(f, n - 1, 1), pltpu.roll(f, n - 57, 1)
        return jnp.where(col < 7, near, jnp.where(tile < COLS - 1, far, 0.0))
    near, far = pltpu.roll(f, 1, 1), pltpu.roll(f, 57, 1)
    return jnp.where(col > 0, near, jnp.where(tile > 0, far, 0.0))


def shift_rows(f, step):
    if step == 0:
        return f
    n = f.shape[1]
    lane = iota(f.shape, 1)
    row, tile = (lane // 8) % 8, lane // 512
    if step == 1:
        near, far = pltpu.roll(f, n - 8, 1), pltpu.roll(f, n - 456, 1)
        return jnp.where(row < 7, near, jnp.where(tile < ROWS - 1, far, 0.0))
    near, far = pltpu.roll(f, 8, 1), pltpu.roll(f, 456, 1)
    return jnp.where(row > 0, near, jnp.where(tile > 0, far, 0.0))


INPUTS = dict(
    fld=(NT * NT, 4, ITEMS),
    ct=(PTS, D),
    wc=(9, 4, D),
    cb=(1, D),
    g1=(1, D),
    s1=(1, D),
    wq=(D, D),
    wk=(D, D),
    wv=(D, D),
    wo=(D, D),
    g2=(1, D),
    s2=(1, D),
    wh=(D, 512),
    bh=(1, 512),
    wr=(512, D),
    br=(1, D),
    dq=(128, D),
    dk=(D, D),
    dv=(D, D),
    do=(D, D),
    wu=(D, 512),
    bu=(1, 512),
    wd=(512, D),
    ps=(1, D),
)


def kernel(*refs):
    gs, *refs = refs
    args, refs = refs[: len(INPUTS)], refs[len(INPUTS) :]
    o_res, o_fg, o_g, *refs = refs
    R = types.SimpleNamespace(**dict(zip([*SCRATCH, *INPUTS], refs, strict=True)))
    G = R.G
    row, col = lax.axis_index("row"), lax.axis_index("col")
    me = row * COLS + col
    core, xbit, ybit = col % 2, (col // 2) % 2, col // 4
    item = me // 2

    def at(number):
        return (number // COLS, number % COLS)

    def remote(src, dst, send, recv, to):
        copy = pltpu.make_async_remote_copy(
            src_ref=src, dst_ref=dst, send_sem=send, recv_sem=recv, device_id=to, device_id_type=MESH
        )
        copy.start()
        return copy

    def drain(ref, sem):
        pltpu.make_async_copy(ref, ref, sem).wait()

    def send_or_copy(src, dst, send, recv, number):
        @pl.when(number != me)
        def _():
            remote(src, dst, send, recv, at(number))

        @pl.when(number == me)
        def _():
            pltpu.make_async_copy(src, dst, recv).start()

    loads = {}
    for i, n in enumerate(INPUTS):
        loads[n] = pltpu.make_async_copy(args[i], getattr(R, n), R.s_in.at[i])
        loads[n].start()

    def need(*wanted):
        for n in wanted:
            loads.pop(n).wait()

    barrier = pltpu.get_barrier_semaphore()
    for k in range(1, DEVICES):
        pl.semaphore_signal(
            barrier, inc=1, device_id=at((me + k) % DEVICES), device_id_type=MESH
        )

    need("fld")
    for ch in range(4):
        R.FA[pl.ds(ch, ITEMS, stride=8), pl.ds(0, 64)] = jnp.transpose(R.fld[:, ch, :])
    size_r, size_c = gs[0, item], gs[1, item]
    fr, fc = size_r.astype(f32), size_c.astype(f32)

    def rotary_tables():
        shape = (80, 128)
        k, lane = iota(shape, 0), iota(shape, 1)
        is_x = k < 16
        coord = jnp.where(
            is_x,
            ((16 * core + k).astype(f32) + 0.5) / fr,
            ((k - 16).astype(f32) + 0.5) / fc,
        )
        freq = (lane % 8 + 1).astype(f32)
        quarter = (lane // 8) % 4
        keep = is_x == (quarter < 2)
        turns = freq * coord
        turns = turns - jnp.round(turns)
        cos_t = jnp.where(keep, turn_sin(turns + 0.25), 0.0)
        sin_t = jnp.where(keep, turn_sin(turns), 0.0)
        sin_t = jnp.where(quarter % 2 == 0, -sin_t, sin_t)
        p, t = iota((PTS, 80), 0), iota((PTS, 80), 1)
        pick = (t == 8 * (p // 512) + (p // 8) % 8) | (t - 16 == 8 * ((p // 64) % 8) + p % 8)
        R.rot[...] = dot_mark(
            pick.astype(jnp.bfloat16), jnp.concatenate([cos_t, sin_t], axis=1), 1
        )

    def fourier_tables():
        shape = (96, 128)
        k, lane = iota(shape, 0), iota(shape, 1)
        is_x = k < 32
        coord = jnp.where(is_x, (k.astype(f32) + 0.5) / fr, ((k - 32).astype(f32) + 0.5) / fc)
        turns = 0.5 * ((lane % 32 + 1).astype(f32) * coord)
        turns = turns - jnp.round(turns)
        turns = jnp.where((lane // 32) % 2 == 0, turns, turns + 0.25)
        R.FF[...] = jnp.where(is_x == (lane < 64), turn_sin(turns), 0.0)

    def tile_masks():
        p = iota((PTS, 128), 0)
        here_r = 16 * core + 8 * (p // 512) + (p // 8) % 8
        here_c = 8 * ((p // 64) % 8) + p % 8
        inv_points = 1.0 / (fr * fc)
        R.wgt[...] = jnp.where((here_r < size_r) & (here_c < size_c), inv_points, 0.0)
        for b in range(ITEMS):
            p = iota((64, 128), 0)
            ok = (NT * row + (p // 8) % 8 < gs[0, b]) & (NT * col + p % 8 < gs[1, b])
            R.mask[pl.ds(64 * b, 64)] = ok.astype(f32)
        p, t = iota((PTS, D), 0), iota((PTS, D), 1)
        chosen = (p // 64 == t // 16) & (
            ((t % 16) == (p // 8) % 8) | ((t % 16) == 8 + p % 8)
        )
        R.E[...] = chosen.astype(jnp.bfloat16)

    rotary_tables()
    fourier_tables()
    tile_masks()
    need("ct", "wd")
    mask2 = jnp.concatenate([R.mask[...]] * 2, axis=1)
    R.ctm[...] = R.ct[...] * mask2
    need("wc")
    R.W9[...] = jnp.zeros((72, D), f32)
    for k in range(9):
        R.W9[pl.ds(8 * k, 4)] = R.wc[k]
    pl.semaphore_wait(barrier, DEVICES - 1)

    for k in range(1, DEVICES):
        to = (me + k) % DEVICES
        remote(
            R.FA.at[pl.ds((to // 2) * 8, 4)],
            R.FR.at[pl.ds(me * 8, 4)],
            R.s_f.at[0],
            R.r_f.at[0],
            at(to),
        )
    R.FR[pl.ds(me * 8, 4)] = R.FA[pl.ds(item * 8, 4)]

    R.dact[...] = nt(R.ctm[...], R.wd[...])
    R.rcc[...] = dot_mark(R.E[...], R.ctm[...], 0)
    ps_grad = colsum(R.ctm[...])

    def cossin():
        c, s = R.rot[:, :128], R.rot[:, 128:]
        return jnp.concatenate([c, c], axis=1), jnp.concatenate([s, s], axis=1)

    def turn(v):
        c, s = cossin()
        return v * c + swap_pairs(v) * s

    def turn_back(v):
        c, s = cossin()
        return v * c - swap_pairs(v) * s

    def wgt2():
        return jnp.concatenate([R.wgt[...]] * 2, axis=1)

    need(*list(loads))
    R.FQ[...] = nn(R.FF[...], R.dq[...])
    drain(R.FR.at[pl.ds(0, 4 * (DEVICES - 1))], R.r_f.at[0])
    lane, sub = iota((8, DEVICES * 64), 1), iota((8, DEVICES * 64), 0)
    full_r, full_c = 8 * (lane // 512) + (lane // 8) % 8, 8 * ((lane // 64) % 8) + lane % 8
    full_mask = (full_r < size_r) & (full_c < size_c) & (sub < 4)
    low = iota((8, 128), 1) < 64
    pieces = []
    for k in range(DEVICES // 2):
        left = R.FR[pl.ds(16 * k, 8)]
        right = R.FR[pl.ds(16 * k + 8, 8)]
        pieces.append(jnp.where(low, left, pltpu.roll(right, 64, 1)))
    field = jnp.where(full_mask, jnp.concatenate(pieces, axis=1), 0.0)
    for dj in range(3):
        along = shift_cols(field, dj - 1)
        for di in range(3):
            patch = shift_rows(along, di - 1)
            mine = jnp.where(core == 0, patch[:, :PTS], patch[:, PTS:])
            R.PT[pl.ds((di * 3 + dj) * 8, 8)] = mine

    hidden0 = tn(R.PT[...], R.W9[...]) + R.cb[...]
    R.h0[...] = hidden0
    mean = jnp.mean(hidden0, axis=-1, keepdims=True)
    center = hidden0 - mean
    rstd1 = lax.rsqrt(jnp.mean(center * center, axis=-1, keepdims=True) + 1e-5)
    R.rs1[...] = jnp.broadcast_to(rstd1, (PTS, 128))
    R.n1[...] = center * rstd1
    R.n[...] = R.n1[...] * R.g1[...] + R.s1[...]
    R.k[...] = turn(nn(R.n[...], R.wk[...]))
    R.wn[...] = R.n[...] * wgt2()
    R.T[...] = tn(R.k[...], R.wn[...])

    pair = (row, col + 1 - 2 * core)

    def swap_start(i, value):
        R.XS[i] = value
        return remote(R.XS.at[i], R.XR.at[i], R.s_x.at[i], R.r_x.at[i], pair)

    def swap_end(i, copy):
        copy.wait()
        return R.XS[i] + R.XR[i]

    going = swap_start(0, compact(nn(R.T[...], R.wv[...])))
    R.q[...] = turn(nn(R.n[...], R.wq[...]))
    R.KV[...] = expand(swap_end(0, going))
    R.KVO[...] = nn(R.KV[...], R.wo[...])
    hidden1 = R.h0[...] + nn(R.q[...], R.KVO[...])
    mean = jnp.mean(hidden1, axis=-1, keepdims=True)
    center = hidden1 - mean
    rstd2 = lax.rsqrt(jnp.mean(center * center, axis=-1, keepdims=True) + 1e-5)
    R.rs2[...] = jnp.broadcast_to(rstd2, (PTS, 128))
    R.m1[...] = center * rstd2
    R.m[...] = R.m1[...] * R.g2[...] + R.s2[...]
    R.h1[...] = hidden1 + R.br[...]
    z = nn(R.m[...], R.wh[...]) + R.bh[...]
    R.az[...] = z
    R.a[...] = jax.nn.gelu(z, approximate=True)
    R.h2[...] = R.h1[...] + nn(R.a[...], R.wr[...])
    R.gram[...] = tn(R.h2[...], R.h2[...] * wgt2())
    half = nn(tn(R.dk[...], R.gram[...]), R.dv[...])
    going = swap_start(1, compact(half))
    R.DS[...] = expand(swap_end(1, going))
    R.AB[...] = nn(nn(R.FQ[...], R.DS[...]), R.do[...])

    for k in range(16):
        R.TS[k, pl.ds(0, 8)] = R.AB[pl.ds(16 * core + 8 * (k // 8), 8)]
        R.TS[k, pl.ds(8, 8)] = R.AB[pl.ds(32 + 8 * (k % 8), 8)]
    for k in range(16):
        slot = (me + k) % 16
        send_or_copy(
            R.TS.at[slot],
            R.TR.at[item],
            R.s_t.at[0],
            R.r_t.at[item],
            16 * core + slot,
        )
    R.az[...] = gelu_both(R.az[...])[1]
    R.X2[...] = nn(R.gram[...], R.dv[...])
    R.P1[...] = nn(R.dq[...], R.DS[...])
    for b in range(ITEMS):
        drain(R.TR.at[b], R.r_t.at[b])

    first, second = (
        xbit * (1 - core) + ybit * core,
        ybit * (1 - core) + xbit * core,
    )
    step_x, step_y = 2 - 4 * xbit, 4 - 8 * ybit
    col_first = col + step_x * (1 - core) + step_y * core
    col_second = col + step_y * (1 - core) + step_x * core

    def sum_chunk(i):
        o, n, kind = CHUNKS[i]
        buf, used, free = R.RB, [SEMS * i], [o]
        place = 2 * ybit + xbit
        half_at = o + core * (n // 2)
        quarter_at = half_at + first * (n // 4)
        eighth_at = quarter_at + second * (n // 8) if kind == AXES else half_at + place * (n // 8)
        shard_at = eighth_at + row * (n // 32)
        plane = [
            (row, col + step_x, 2 * ybit + 1 - xbit),
            (row, col + step_y, 2 * (1 - ybit) + xbit),
            (row, col + step_x + step_y, 2 * (1 - ybit) + 1 - xbit),
        ]
        here = (row, col, place)
        line = [((row + z) % ROWS, col) for z in range(1, ROWS)]

        def part(ref, start, count):
            return ref.at[pl.ds(pl.multiple_of(start, 8), count)]

        def go(src, dst, to):
            copy = remote(src, dst, R.s_g.at[used[0]], R.r_g.at[used[0]], to)
            used[0] += 1
            return copy

        def give(mine, count, *away):
            copies, came = [], []
            for start, to in away:
                here = buf.at[pl.ds(free[0], count)]
                free[0] += count
                came.append(here)
                copies.append(go(part(G, start, count), here, to))

            def add(into):
                for copy in copies:
                    copy.wait()
                total = part(G, mine, count)[...]
                for here in came:
                    total = total + here[...]
                part(into, mine, count)[...] = total

            return add

        def spread(mine, count, *to):
            rows = part(R.SUM, mine, count)
            copies = [go(rows, rows, device) for device in to]

            def wait():
                for copy in copies:
                    copy.wait()

            return wait

        add = give(half_at, n // 2, (o + (1 - core) * (n // 2), pair))
        yield
        add(G)
        if kind == ALL:
            chips = [((row + z) % ROWS, c, p) for z in range(ROWS) for _, c, p in [here, *plane]][1:]
            away = [(half_at + (4 * p + r) * (n // 32), (r, c)) for r, c, p in chips]
            shard_at = half_at + (4 * place + row) * (n // 32)
            add = give(shard_at, n // 32, *away)
            yield
            add(R.SUM)
            wait = spread(shard_at, n // 32, *[(r, c) for r, c, _ in chips])
            yield
            wait()
        elif kind == PLANE:
            away = [(half_at + p * (n // 8), (r, c)) for r, c, p in plane]
            add = give(eighth_at, n // 8, *away)
            yield
            add(G)
        else:
            away = half_at + (1 - first) * (n // 4)
            add = give(quarter_at, n // 4, (away, (row, col_first)))
            yield
            add(G)
            away = quarter_at + (1 - second) * (n // 8)
            add = give(eighth_at, n // 8, (away, (row, col_second)))
            yield
            add(G)
        if kind != ALL:
            away = [(eighth_at + to[0] * (n // 32), to) for to in line]
            add = give(shard_at, n // 32, *away)
            yield
            add(R.SUM)
            wait = spread(shard_at, n // 32, *line)
            yield
            wait()
        if kind == PLANE:
            wait = spread(eighth_at, n // 8, *[(r, c) for r, c, _ in plane])
            yield
            wait()
        elif kind == AXES:
            wait = spread(eighth_at, n // 8, (row, col_second))
            yield
            wait()
            wait = spread(quarter_at, n // 4, (row, col_first))
            yield
            wait()
        wait = spread(half_at, n // 2, pair)
        yield
        wait()
        out = pltpu.make_async_copy(
            R.SUM.at[pl.ds(o, n)], o_g.at[pl.ds(o, n)], R.s_o.at[1 + i]
        )
        out.start()
        outs.append(out)

    going_on, outs, plan = {}, [], list(PLAN)

    def launch(*ready):
        for i, chunk in enumerate(CHUNKS):
            if chunk[0] in ready:
                going_on[i] = sum_chunk(i)
                next(going_on[i])
        step()

    def advance(i):
        if next(going_on[i], i) == i:
            del going_on[i]

    def step():
        for i in plan.pop(0):
            advance(i)

    table = R.TR[...].reshape(ITEMS * 16, D)
    R.UT[...] = nn(table, R.wu[...])
    a, slope = gelu_both(dot_mark(R.E[...], R.UT[...], 1) + R.bu[...])
    R.act[...] = a
    R.dpre[...] = slope * R.dact[...]
    R.rc[...] = dot_mark(R.E[...], R.dpre[...], 0)
    R.DAB[...] = (nt(R.rc[...], R.wu[...]) + R.rcc[...]).reshape(ITEMS, 16, D)
    for k in range(ITEMS):
        b = (item + k) % ITEMS
        send_or_copy(
            R.DAB.at[b],
            R.DR.at[me % 16],
            R.s_r.at[0],
            R.r_r.at[me % 16],
            2 * b + row // 2,
        )
    table = R.TR[...].reshape(ITEMS * 16, D)
    grad = tn(table, R.rc[...])
    G[pl.ds(R_UP, D)] = grad[:, :D]
    G[pl.ds(R_UP + D, D)] = grad[:, D:]
    launch(R_UP)
    G[pl.ds(R_DOWN, 512)] = tn(R.act[...], R.ctm[...])
    step()
    launch(R_DOWN)
    latent = dot_mark(R.E[...], table, 1)
    mask2 = jnp.concatenate([R.mask[...]] * 2, axis=1)
    R.res[...] = (latent + nn(R.act[...], R.wd[...]) + R.ps[...]) * mask2
    out_res = pltpu.make_async_copy(R.res, o_res, R.s_o.at[0])
    out_res.start()
    bu_grad = colsum(R.dpre[...])
    step()

    for k in range(16):
        drain(R.DR.at[k], R.r_r.at[k])
    step()
    da = [jnp.zeros((8, D), f32) for _ in range(2)]
    db = []
    for t in range(COLS):
        for s in range(2):
            da[s] = da[s] + R.DR[s * 8 + t, pl.ds(0, 8)]
        db.append(R.DR[t, pl.ds(8, 8)] + R.DR[8 + t, pl.ds(8, 8)])
    zero = jnp.zeros((8, D), f32)
    is0 = core == 0
    dab = jnp.concatenate(
        [
            jnp.where(is0, da[0], zero),
            jnp.where(is0, da[1], zero),
            jnp.where(is0, zero, da[0]),
            jnp.where(is0, zero, da[1]),
            *db,
        ],
        axis=0,
    )
    going = swap_start(2, compact(tn(R.FQ[...], nt(dab, R.do[...]))))
    dm_table = tn(R.FF[...], dab)
    step()
    G[pl.ds(R_DO, D)] = tn(R.P1[...], dm_table)
    R.DP[...] = nt(dm_table, R.do[...])
    step()
    step()
    step()
    dd = expand(swap_end(2, going))
    step()
    y1 = nn(R.dk[...], dd)
    dgram = nt(y1, R.dv[...]) + nt(R.dv[...], y1)
    step()
    R.dh[...] = nn(R.h2[...], dgram) * wgt2()
    step()
    G[pl.ds(R_DK, D)] = nt(R.X2[...], dd)
    G[pl.ds(R_DV, D)] = tn(R.gram[...], y1)
    step()
    launch(R_DO)
    br_grad = colsum(R.dh[...])
    G[pl.ds(R_RET, 512)] = tn(R.a[...], R.dh[...])
    step()
    launch(R_RET)
    R.dz[...] = nt(R.dh[...], R.wr[...]) * R.az[...]
    bh_grad = colsum(R.dz[...])
    step()
    grad = tn(R.m[...], R.dz[...])
    G[pl.ds(R_HID, D)] = grad[:, :D]
    G[pl.ds(R_HID + D, D)] = grad[:, D:]
    step()
    launch(R_HID)
    dm = nt(R.dz[...], R.wh[...])
    step()
    g2_grad, s2_grad = colsum(dm * R.m1[...]), colsum(dm)
    rs2 = jnp.concatenate([R.rs2[...]] * 2, axis=1)
    R.dh[...] = R.dh[...] + norm_back(dm * R.g2[...], R.m1[...], rs2)
    step()
    stat = tn(R.q[...], R.dh[...])
    going = swap_start(3, compact(nt(stat, R.wo[...])))
    step()
    G[pl.ds(R_O, D)] = tn(R.KV[...], stat)
    R.dq0[...] = turn_back(nt(R.dh[...], R.KVO[...]))
    step()
    G[pl.ds(R_Q, D)] = tn(R.n[...], R.dq0[...])
    step()
    launch(R_O, R_Q)
    dkv = expand(swap_end(3, going))
    G[pl.ds(R_V, D)] = tn(R.T[...], dkv)
    step()
    launch(R_V)
    dt = nt(dkv, R.wv[...])
    R.dk0[...] = turn_back(nt(R.wn[...], dt))
    step()
    G[pl.ds(R_K, D)] = tn(R.n[...], R.dk0[...])
    step()
    launch(R_K)
    dn = (
        nn(R.k[...], dt) * wgt2()
        + nt(R.dq0[...], R.wq[...])
        + nt(R.dk0[...], R.wk[...])
    )
    step()
    g1_grad, s1_grad = colsum(dn * R.n1[...]), colsum(dn)
    rs1 = jnp.concatenate([R.rs1[...]] * 2, axis=1)
    R.dh[...] = R.dh[...] + norm_back(dn * R.g1[...], R.n1[...], rs1)
    step()

    cb_grad = colsum(R.dh[...])
    conv_grad = nn(R.PT[...], R.dh[...])
    vectors = [
        cb_grad, g1_grad, s1_grad, g2_grad, s2_grad, br_grad, ps_grad,
        bh_grad[:, :D], bh_grad[:, D:], bu_grad[:, :D], bu_grad[:, D:],
    ]
    vectors.append(jnp.zeros((128 - S_VEC - len(vectors), D), f32))
    G[pl.ds(R_SMALL, 128)] = jnp.concatenate([conv_grad, *vectors], axis=0)
    G[pl.ds(R_DQ, 128)] = nt(R.DP[...], R.DS[...])
    launch(R_DQ)
    dpt = nt(R.W9[...], R.dh[...])
    half_lane = iota((8, 2 * PTS), 1) // PTS == core
    back = jnp.zeros((8, 2 * PTS), f32)
    for di in range(3):
        line = jnp.zeros((8, 2 * PTS), f32)
        for dj in range(3):
            part = dpt[(di * 3 + dj) * 8 : (di * 3 + dj) * 8 + 8]
            part = jnp.where(half_lane, jnp.concatenate([part, part], axis=1), 0.0)
            line = line + shift_cols(part, 1 - dj)
        back = back + shift_rows(line, 1 - di)
    back = jnp.where(full_mask, back, 0.0)
    for k in range(DEVICES // 2):
        R.FS[pl.ds(8 * k, 8)] = back[:, 128 * k : 128 * (k + 1)]
    for k in range(1, DEVICES):
        to = (me + k) % DEVICES
        remote(
            R.FS.at[pl.ds((to // 2) * 8, 4)],
            R.FB.at[pl.ds(me * 8, 4)],
            R.s_b.at[0],
            R.r_b.at[0],
            at(to),
        )
    R.FB[pl.ds(me * 8, 4)] = R.FS[pl.ds(item * 8, 4)]
    step()

    def field_end():
        drain(R.FB.at[pl.ds(0, 4 * (DEVICES - 1))], R.r_b.at[0])
        for b in range(ITEMS):
            both = R.FB[pl.ds(16 * b, 8)] + R.FB[pl.ds(16 * b + 8, 8)]
            R.FO[pl.ds(8 * b, 8)] = jnp.where(core == 0, both, pltpu.roll(both, 64, 1))
        out = pltpu.make_async_copy(R.FO, o_fg, R.s_o.at[len(CHUNKS) + 1])
        out.start()
        outs.append(out)

    for i in TAIL:
        if i < 0:
            field_end()
        else:
            advance(i)
    assert not going_on and not plan

    drain(R.FR.at[pl.ds(0, 4 * (DEVICES - 1))], R.s_f.at[0])
    drain(R.FB.at[pl.ds(0, 4 * (DEVICES - 1))], R.s_b.at[0])
    inside_t = core == row // 2

    @pl.when(inside_t)
    def _():
        drain(R.TS.at[pl.ds(0, 15)], R.s_t.at[0])
        drain(R.DAB.at[pl.ds(0, 15)], R.s_r.at[0])

    @pl.when(jnp.logical_not(inside_t))
    def _():
        drain(R.TS, R.s_t.at[0])
        drain(R.DAB, R.s_r.at[0])

    out_res.wait()
    for out in outs:
        out.wait()


def vmem(*shape):
    return pltpu.VMEM(shape, f32)


SCRATCH = dict(
    G=vmem(G_ROWS, D),
    RB=vmem(G_ROWS, D),
    SUM=vmem(G_ROWS, D),
    FA=vmem(ITEMS * 8, 128),
    FR=vmem(DEVICES * 8, 128),
    FS=vmem(ITEMS * 8, 128),
    FB=vmem(DEVICES * 8, 128),
    FO=vmem(ITEMS * 8, 128),
    DP=vmem(128, D),
    FQ=vmem(96, D),
    W9=vmem(72, D),
    XS=vmem(4, HEAD, D),
    XR=vmem(4, HEAD, D),
    TS=vmem(16, 16, D),
    TR=vmem(ITEMS, 16, D),
    DAB=vmem(ITEMS, 16, D),
    DR=vmem(16, 16, D),
    mask=vmem(PTS, 128),
    wgt=vmem(PTS, 128),
    ctm=vmem(PTS, D),
    E=pltpu.VMEM((PTS, D), jnp.bfloat16),
    dact=vmem(PTS, 512),
    rcc=vmem(256, D),
    rc=vmem(256, 512),
    rot=vmem(PTS, D),
    FF=vmem(96, 128),
    PT=vmem(72, PTS),
    h0=vmem(PTS, D),
    rs1=vmem(PTS, 128),
    n1=vmem(PTS, D),
    n=vmem(PTS, D),
    wn=vmem(PTS, D),
    q=vmem(PTS, D),
    k=vmem(PTS, D),
    T=vmem(D, D),
    KV=vmem(D, D),
    KVO=vmem(D, D),
    rs2=vmem(PTS, 128),
    m1=vmem(PTS, D),
    m=vmem(PTS, D),
    h1=vmem(PTS, D),
    a=vmem(PTS, 512),
    az=vmem(PTS, 512),
    h2=vmem(PTS, D),
    gram=vmem(D, D),
    DS=vmem(D, D),
    P1=vmem(128, D),
    X2=vmem(D, D),
    AB=vmem(96, D),
    UT=vmem(256, 512),
    act=vmem(PTS, 512),
    dpre=vmem(PTS, 512),
    res=vmem(PTS, D),
    dh=vmem(PTS, D),
    dz=vmem(PTS, 512),
    dq0=vmem(PTS, D),
    dk0=vmem(PTS, D),
    s_in=pltpu.SemaphoreType.DMA((len(INPUTS),)),
    s_f=pltpu.SemaphoreType.DMA((1,)),
    r_f=pltpu.SemaphoreType.DMA((1,)),
    s_b=pltpu.SemaphoreType.DMA((1,)),
    r_b=pltpu.SemaphoreType.DMA((1,)),
    s_t=pltpu.SemaphoreType.DMA((1,)),
    r_t=pltpu.SemaphoreType.DMA((16,)),
    s_r=pltpu.SemaphoreType.DMA((1,)),
    r_r=pltpu.SemaphoreType.DMA((16,)),
    s_x=pltpu.SemaphoreType.DMA((4,)),
    r_x=pltpu.SemaphoreType.DMA((4,)),
    s_g=pltpu.SemaphoreType.DMA((SEMS * len(CHUNKS),)),
    r_g=pltpu.SemaphoreType.DMA((SEMS * len(CHUNKS),)),
    s_o=pltpu.SemaphoreType.DMA((2 + len(CHUNKS),)),
)

PARTS = dict(
    wc=(9, 4, D),
    cb=(1, D),
    g1=(1, D),
    s1=(1, D),
    wq=(D, D),
    wk=(D, D),
    wv=(D, D),
    wo=(D, D),
    g2=(1, D),
    s2=(1, D),
    wh=(D, 512),
    bh=(1, 512),
    wr=(512, D),
    br=(1, D),
    dq=(128, D),
    dk=(D, D),
    dv=(D, D),
    do=(D, D),
    wu=(D, 512),
    bu=(1, 512),
    wd=(512, D),
    ps=(1, D),
)
ROW_AT = dict(
    wq=R_Q, wk=R_K, wv=R_V, wo=R_O, wr=R_RET, dq=R_DQ, dk=R_DK, dv=R_DV, do=R_DO, wd=R_DOWN,
    wh=R_HID, wu=R_UP,
)


SMALL_PARTS = tuple(name for name in PARTS if name not in ROW_AT)


def unpack(res_in, fg_in, g_in, res_out, fg_out, *rest):
    outs = dict(zip(PARTS, rest[: len(PARTS)], strict=True))
    res, fg, g, sem_in, sem_out, fg_here, *here = rest[len(PARTS) :]
    staged = dict(zip(SMALL_PARTS, here, strict=True))
    moves = []

    def add(src, here, *out):
        load = pltpu.make_async_copy(src, here, sem_in.at[len(moves)])
        load.start()
        moves.append((load, out))

    add(g_in.at[pl.ds(R_SMALL, 128)], g.at[pl.ds(R_SMALL, 128)])
    add(fg_in, fg)
    for k in range(4):
        part = pl.ds(k * 256, 256)
        add(res_in.at[part], res.at[part], (res.at[part], res_out.at[part]))
    for name, start in ROW_AT.items():
        count = 512 if name in ("wh", "wu") else PARTS[name][0]
        here = g.at[pl.ds(start, count)]
        if name in ("wh", "wu"):
            out = [
                (g.at[pl.ds(start + s * D, D)], outs[name].at[:, pl.ds(s * D, D)])
                for s in range(2)
            ]
        else:
            out = [(here, outs[name])]
        add(g_in.at[pl.ds(start, count)], here, *out)
    stores = []

    def store(src, dst):
        stores.append(pltpu.make_async_copy(src, dst, sem_out.at[len(stores)]))
        stores[-1].start()

    moves[0][0].wait()
    for k in range(9):
        line = R_SMALL + S_CONV + 8 * k
        staged["wc"][k] = g[line : line + 4]
    line = R_SMALL + S_VEC
    for name in VECS:
        for k in range(PARTS[name][1] // D):
            staged[name][:, D * k : D * (k + 1)] = g[line : line + 1]
            line += 1
    for name in SMALL_PARTS:
        store(staged[name], outs[name])
    moves[1][0].wait()
    for ch in range(4):
        fg_here[:, ch, :] = jnp.transpose(fg[pl.ds(ch, ITEMS, stride=8), pl.ds(0, 64)])
    store(fg_here, fg_out)
    for load, out in moves[2:]:
        load.wait()
        for src, dst in out:
            store(src, dst)
    for out in stores:
        out.wait()


ARGUMENTS = tuple(n for n in INPUTS if n not in ("fld", "ct"))


def item_body(field_in, *rest):
    values = dict(zip(ARGUMENTS + ("ct", "gs"), rest, strict=True))
    values["fld"] = field_in.transpose(1, 2, 3, 0)
    operands = [values["gs"].T]
    operands += [values[name].reshape(shape) for name, shape in INPUTS.items()]
    in_smem = pl.BlockSpec(memory_space=pltpu.SMEM)
    anywhere = pl.BlockSpec(memory_space=pl.ANY)
    made = pl.pallas_call(
        kernel,
        out_shape=(
            jax.ShapeDtypeStruct((PTS, D), f32),
            jax.ShapeDtypeStruct((ITEMS * 8, 128), f32),
            jax.ShapeDtypeStruct((G_ROWS, D), f32),
        ),
        in_specs=[in_smem] + [anywhere] * len(INPUTS),
        out_specs=(anywhere,) * 3,
        scratch_shapes=[*SCRATCH.values()] + [vmem(*shape) for shape in INPUTS.values()],
        compiler_params=pltpu.CompilerParams(
            collective_id=1, has_side_effects=True, vmem_limit_bytes=60 * 2**20
        ),
        name="layer",
    )(*operands)
    outs = pl.pallas_call(
        unpack,
        out_shape=(
            jax.ShapeDtypeStruct((PTS, D), f32),
            jax.ShapeDtypeStruct((NT * NT, 4, ITEMS), f32),
            *(jax.ShapeDtypeStruct(shape, f32) for shape in PARTS.values()),
        ),
        in_specs=[anywhere] * 3,
        out_specs=(anywhere,) * (2 + len(PARTS)),
        scratch_shapes=[
            vmem(PTS, D),
            vmem(ITEMS * 8, 128),
            vmem(G_ROWS, D),
            pltpu.SemaphoreType.DMA((24,)),
            pltpu.SemaphoreType.DMA((40,)),
            vmem(NT * NT, 4, ITEMS),
            *(vmem(*PARTS[name]) for name in SMALL_PARTS),
        ],
        compiler_params=pltpu.CompilerParams(vmem_limit_bytes=60 * 2**20),
        name="unpack",
    )(*made)
    shaped = []
    for name, value in zip(PARTS, outs[2:], strict=True):
        if name == "wc":
            value = value.reshape(3, 3, 4, D)
        elif name in VECS:
            value = value.reshape(-1)
        shaped.append(value)
    return (
        outs[0].reshape(ITEMS, NT, NT, D),
        outs[1].reshape(NT, NT, 4, ITEMS).transpose(3, 0, 1, 2),
        *shaped,
    )


def body(field_in, *rest):
    tile = field_in.shape[:3]
    mesh = (lax.axis_size("row"), lax.axis_size("col"))
    if mesh == (ROWS, COLS) and tile == (ITEMS, NT, NT):
        return item_body(field_in, *rest)
    return general_body(field_in, *rest)


def solution(mesh):
    spread = P(None, "row", "col", None)
    placed = (spread,) + (P(),) * 22 + (spread, P())
    return jax.shard_map(
        body,
        mesh=mesh,
        in_specs=placed,
        out_specs=(spread, spread) + (P(),) * 22,
        check_vma=False,
    )
```

```python
import math
import types

import jax
import jax.numpy as jnp
from jax import lax
from jax.experimental import pallas as pl
from jax.experimental.pallas import tpu as pltpu
from jax.sharding import PartitionSpec as P

HEADS = 8
HEAD = 32
FOUR = 128

highest = lax.Precision.HIGHEST
f32 = jnp.float32
MESH = pl.DeviceIdType.MESH


def padded_2(x, sides, width):
    for axis, dim in sides:
        size, length = (lax.axis_size(axis), x.shape[dim])
        up = [(i, (i + 1) % size) for i in range(size - 1)]
        down = [(j, i) for i, j in up]
        last = lax.slice_in_dim(x, length - width, length, axis=dim)
        leading = lax.slice_in_dim(x, 0, width, axis=dim)
        before = lax.ppermute(last, axis, up)
        after = lax.ppermute(leading, axis, down)
        x = jnp.concatenate([before, x, after], axis=dim)
    return x


def matmul(left, right):
    return jnp.matmul(left, right, precision=highest)


def smooth(values):
    return jax.nn.gelu(values, approximate=True)


def layer_norm(values, norm_gain, norm_shift):
    average = jnp.mean(values, axis=-1, keepdims=True)
    center = values - average
    spread = jnp.mean(center * center, axis=-1, keepdims=True)
    return center * lax.rsqrt(spread + 1e-05) * norm_gain + norm_shift


def geometry(row_index, col_index, grid_sizes):
    size_rows = grid_sizes[:, 0]
    size_cols = grid_sizes[:, 1]
    within = (row_index[None, :, None] < size_rows[:, None, None]) & (
        col_index[None, None, :] < size_cols[:, None, None]
    )
    inside = within.astype(jnp.float32)
    coord_x = (row_index.astype(jnp.float32)[None, :, None] + 0.5) / size_rows.astype(jnp.float32)[
        :, None, None
    ] + 0.0 * inside
    coord_y = (col_index.astype(jnp.float32)[None, None, :] + 0.5) / size_cols.astype(jnp.float32)[
        :, None, None
    ] + 0.0 * inside
    points = (size_rows * size_cols).astype(jnp.float32)
    return (inside, coord_x, coord_y, points)


def features(coord_x, coord_y):
    angles = math.pi * (jnp.arange(FOUR // 4).astype(jnp.float32) + 1.0)
    along_x = coord_x[..., None] * angles
    along_y = coord_y[..., None] * angles
    return jnp.concatenate(
        [jnp.sin(along_x), jnp.cos(along_x), jnp.sin(along_y), jnp.cos(along_y)], axis=-1
    )


def rotate(vectors, coord_x, coord_y):
    quarter = HEAD // 4
    angles = 2.0 * math.pi * (jnp.arange(quarter).astype(jnp.float32) + 1.0)
    turn_x = coord_x[..., None, None] * angles
    turn_y = coord_y[..., None, None] * angles
    cosine_x, sine_x = (jnp.cos(turn_x), jnp.sin(turn_x))
    cosine_y, sine_y = (jnp.cos(turn_y), jnp.sin(turn_y))
    part_one = vectors[..., :quarter]
    part_two = vectors[..., quarter : 2 * quarter]
    part_three = vectors[..., 2 * quarter : 3 * quarter]
    part_four = vectors[..., 3 * quarter :]
    return jnp.concatenate(
        [
            part_one * cosine_x - part_two * sine_x,
            part_one * sine_x + part_two * cosine_x,
            part_three * cosine_y - part_four * sine_y,
            part_three * sine_y + part_four * cosine_y,
        ],
        axis=-1,
    )


def split_heads(values):
    return values.reshape(values.shape[:-1] + (HEADS, HEAD))


def conv_embed(padded, weight_in, bias_in):
    tile_rows = padded.shape[1] - 2
    tile_cols = padded.shape[2] - 2
    total = jnp.zeros(padded.shape[:1] + (tile_rows, tile_cols, weight_in.shape[-1]), jnp.float32)
    for shift_row in range(3):
        for shift_col in range(3):
            window = padded[
                :, shift_row : shift_row + tile_rows, shift_col : shift_col + tile_cols, :
            ]
            total = total + jnp.einsum(
                "brci,io->brco", window, weight_in[shift_row, shift_col], precision=highest
            )
    return total + bias_in


def conv_transpose(grad_padded, weight_in):
    tile_rows = grad_padded.shape[1] - 2
    tile_cols = grad_padded.shape[2] - 2
    total = jnp.zeros(
        grad_padded.shape[:1] + (tile_rows, tile_cols, weight_in.shape[2]), jnp.float32
    )
    for shift_row in range(3):
        for shift_col in range(3):
            window = grad_padded[
                :,
                2 - shift_row : 2 - shift_row + tile_rows,
                2 - shift_col : 2 - shift_col + tile_cols,
                :,
            ]
            total = total + jnp.einsum(
                "brco,io->brci", window, weight_in[shift_row, shift_col], precision=highest
            )
    return total


def project(params, hidden0, coord_x, coord_y):
    first_gain, first_shift, query_weight, key_weight, value_weight = params
    normed = layer_norm(hidden0, first_gain, first_shift)
    query_heads = rotate(split_heads(matmul(normed, query_weight)), coord_x, coord_y)
    key_heads = rotate(split_heads(matmul(normed, key_weight)), coord_x, coord_y)
    value_heads = split_heads(matmul(normed, value_weight))
    return (query_heads, key_heads, value_heads)


def summary(key_heads, value_heads, weight):
    return jnp.einsum(
        "brchd,brche->bhde", key_heads * weight[..., None, None], value_heads, precision=highest
    )


def encoder_rest(params, hidden0, query_heads, kv_summary):
    (
        output_weight,
        second_gain,
        second_shift,
        hidden_weight,
        hidden_bias,
        return_weight,
        return_bias,
    ) = params
    mixed = jnp.einsum("brchd,bhde->brche", query_heads, kv_summary, precision=highest).reshape(
        hidden0.shape
    )
    hidden1 = hidden0 + matmul(mixed, output_weight)
    normed = layer_norm(hidden1, second_gain, second_shift)
    return (
        hidden1
        + matmul(smooth(matmul(normed, hidden_weight) + hidden_bias), return_weight)
        + return_bias
    )


def decode_summary(params, hidden2, weight):
    decode_key, decode_value = params
    return summary(
        split_heads(matmul(hidden2, decode_key)), split_heads(matmul(hidden2, decode_value)), weight
    )


def decode_out(params, fourier, dec_summary, inside):
    decode_query, decode_output, propagate_up, propagate_bias, propagate_down, propagate_shift = (
        params
    )
    query_heads = split_heads(matmul(fourier, decode_query))
    mixed = jnp.einsum("brchd,bhde->brche", query_heads, dec_summary, precision=highest)
    latent = matmul(mixed.reshape(mixed.shape[:-2] + (HEADS * HEAD,)), decode_output)
    result = (
        latent
        + matmul(smooth(matmul(latent, propagate_up) + propagate_bias), propagate_down)
        + propagate_shift
    )
    return result * inside[..., None]


def general_body(
    field_in,
    conv_weight,
    conv_bias,
    first_gain,
    first_shift,
    query_weight,
    key_weight,
    value_weight,
    output_weight,
    second_gain,
    second_shift,
    hidden_weight,
    hidden_bias,
    return_weight,
    return_bias,
    decode_query,
    decode_key,
    decode_value,
    decode_output,
    propagate_up,
    propagate_bias,
    propagate_down,
    propagate_shift,
    cotangent,
    grid_sizes,
):
    both = ("row", "col")
    tile_rows = field_in.shape[1]
    tile_cols = field_in.shape[2]
    row_index = lax.axis_index("row") * tile_rows + jnp.arange(tile_rows, dtype=jnp.int32)
    col_index = lax.axis_index("col") * tile_cols + jnp.arange(tile_cols, dtype=jnp.int32)
    front_params = (first_gain, first_shift, query_weight, key_weight, value_weight)
    rest_params = (
        output_weight,
        second_gain,
        second_shift,
        hidden_weight,
        hidden_bias,
        return_weight,
        return_bias,
    )
    pair_params = (decode_key, decode_value)
    out_params = (
        decode_query,
        decode_output,
        propagate_up,
        propagate_bias,
        propagate_down,
        propagate_shift,
    )
    inside, coord_x, coord_y, points = geometry(row_index, col_index, grid_sizes)
    fourier = features(coord_x, coord_y)
    weight = inside / points[:, None, None]
    padded = padded_2(field_in * inside[..., None], (("row", 1), ("col", 2)), 1)
    hidden0 = conv_embed(padded, conv_weight, conv_bias)
    query_heads, key_heads, value_heads = project(front_params, hidden0, coord_x, coord_y)
    kv_summary = lax.psum(summary(key_heads, value_heads, weight), both)
    hidden2 = encoder_rest(rest_params, hidden0, query_heads, kv_summary)
    dec_summary = lax.psum(decode_summary(pair_params, hidden2, weight), both)

    def decode_local(params, summary_in):
        return decode_out(params, fourier, summary_in, inside)

    result, out_back = jax.vjp(decode_local, out_params, dec_summary)
    out_grads, dec_part = out_back(cotangent)
    dec_grad = lax.psum(dec_part, both)

    def pair_local(params, hidden_in):
        return decode_summary(params, hidden_in, weight)

    pair_grads, hidden2_grad = jax.vjp(pair_local, pair_params, hidden2)[1](dec_grad)
    rest_back = jax.vjp(encoder_rest, rest_params, hidden0, query_heads, kv_summary)[1]
    rest_grads, hidden0_part, query_grad, kv_part = rest_back(hidden2_grad)
    kv_grad = lax.psum(kv_part, both)

    def summary_local(key_in, value_in):
        return summary(key_in, value_in, weight)

    key_grad, value_grad = jax.vjp(summary_local, key_heads, value_heads)[1](kv_grad)

    def project_local(params, hidden_in):
        return project(params, hidden_in, coord_x, coord_y)

    front_grads, hidden0_more = jax.vjp(project_local, front_params, hidden0)[1](
        (query_grad, key_grad, value_grad)
    )
    hidden0_grad = hidden0_part + hidden0_more

    def conv_local(weight_in, bias_in):
        return conv_embed(padded, weight_in, bias_in)

    conv_grads = jax.vjp(conv_local, conv_weight, conv_bias)[1](hidden0_grad)
    grad_padded = padded_2(hidden0_grad, (("row", 1), ("col", 2)), 1)
    field_grad = conv_transpose(grad_padded, conv_weight) * inside[..., None]
    totals = lax.psum(
        (
            *conv_grads,
            *front_grads,
            *rest_grads,
            out_grads[0],
            *pair_grads,
            *out_grads[1:],
        ),
        both,
    )
    return (result, field_grad, *totals)


NT = 8
ITEMS = 16
ROWS, COLS = 4, 8
DEVICES = ROWS * COLS
PTS = 1024
D = 256

CHUNKS = ((0, 512, 0), (512, 512, 0), (1024, 768, 0), (1792, 512, 0), (2304, 512, 0), (2816, 512, 0), (3328, 256, 1), (3584, 256, 1), (3840, 256, 1))
R_UP, R_DOWN = 0, 512
R_DO, R_DK, R_DV = 1024, 1280, 1536
R_RET, R_HID, R_O, R_Q, R_V, R_K = 1792, 2304, 2816, 3072, 3328, 3584
R_DQ, R_SMALL = 3840, 3968
G_ROWS = 4096
VECS = ("cb", "g1", "s1", "g2", "s2", "br", "ps", "bh", "bu")
S_CONV, S_VEC = 0, 72
PLAN = ((), (), (0, 1), (0,), (), (), (), (1,), (), (), (), (), (), (), (), (0,), (3,), (), (1, 2), (), (4,), (), (), (), (3, 0), (2,), (1, 4), (), (6, 5, 3, 2), (4,), (7,), (0, 1, 3, 6), (5,), ())
TAIL = (1, 8, 6, 3, 7, 0, 5, 2, 3, 7, 6, 4, 5, 2, 0, 7, 8, 4, 2, -1, 5, 4, 3, 6, 8, 5, 1, 8, 2, 7, 7, 4, 5, 6, 0, 8, 3, 2, 4, 1, 5, 8)
AXES, PLANE, ALL = range(3)
SEMS = 32


def dot(a, b, ca, cb):
    return lax.dot_general(a, b, (((ca,), (cb,)), ((), ())), preferred_element_type=f32)


def cut(x):
    top = x.astype(jnp.bfloat16)
    return top, (x - top.astype(f32)).astype(jnp.bfloat16)


def dot3(a, b, ca, cb):
    (a0, a1), (b0, b1) = cut(a), cut(b)
    return dot(a0, b0, ca, cb) + (dot(a0, b1, ca, cb) + dot(a1, b0, ca, cb))


def nn(a, b):
    return dot3(a, b, 1, 0)


def nt(a, b):
    return dot3(a, b, 1, 1)


def tn(a, b):
    return dot3(a, b, 0, 0)


def dot_mark(e, b, ca):
    b0, b1 = cut(b)
    return dot(e, b0, ca, 0) + dot(e, b1, ca, 0)


def iota(shape, dim):
    return lax.broadcasted_iota(jnp.int32, shape, dim)


GC = math.sqrt(2.0 / math.pi)


def gelu_both(x):
    x2 = x * x
    t = jnp.tanh(GC * (x + 0.044715 * (x2 * x)))
    half = 0.5 * (1.0 + t)
    slope = half + 0.5 * x * (1.0 - t * t) * (GC + (3 * 0.044715 * GC) * x2)
    return x * half, slope


def turn_sin(u):
    return jnp.sin((2.0 * math.pi) * (u - jnp.round(u)))


def compact(z):
    lane = iota((HEAD, D), 1) // HEAD
    total = jnp.zeros((HEAD, D), f32)
    for h in range(HEADS):
        total = total + jnp.where(lane == h, z[h * HEAD : (h + 1) * HEAD, :], 0.0)
    return total


def expand(blocks):
    lane = iota((HEAD, D), 1) // HEAD
    return jnp.concatenate([jnp.where(lane == h, blocks, 0.0) for h in range(HEADS)], axis=0)


def swap_pairs(v):
    parts = []
    for s in range(D // 128):
        part = v[:, s * 128 : (s + 1) * 128]
        low = (iota(part.shape, 1) // 8) % 2 == 0
        parts.append(jnp.where(low, pltpu.roll(part, 120, 1), pltpu.roll(part, 8, 1)))
    return jnp.concatenate(parts, axis=1)


def norm_back(dn, nhat, rstd):
    a = jnp.mean(dn, axis=-1, keepdims=True)
    b = jnp.mean(dn * nhat, axis=-1, keepdims=True)
    return rstd * (dn - a - nhat * b)


def colsum(v):
    return jnp.sum(v, axis=0, keepdims=True)


def shift_cols(f, step):
    if step == 0:
        return f
    n = f.shape[1]
    lane = iota(f.shape, 1)
    col, tile = lane % 8, (lane // 64) % 8
    if step == 1:
        near, far = pltpu.roll(f, n - 1, 1), pltpu.roll(f, n - 57, 1)
        return jnp.where(col < 7, near, jnp.where(tile < COLS - 1, far, 0.0))
    near, far = pltpu.roll(f, 1, 1), pltpu.roll(f, 57, 1)
    return jnp.where(col > 0, near, jnp.where(tile > 0, far, 0.0))


def shift_rows(f, step):
    if step == 0:
        return f
    n = f.shape[1]
    lane = iota(f.shape, 1)
    row, tile = (lane // 8) % 8, lane // 512
    if step == 1:
        near, far = pltpu.roll(f, n - 8, 1), pltpu.roll(f, n - 456, 1)
        return jnp.where(row < 7, near, jnp.where(tile < ROWS - 1, far, 0.0))
    near, far = pltpu.roll(f, 8, 1), pltpu.roll(f, 456, 1)
    return jnp.where(row > 0, near, jnp.where(tile > 0, far, 0.0))


INPUTS = dict(
    fld=(NT * NT, 4, ITEMS),
    ct=(PTS, D),
    wc=(9, 4, D),
    cb=(1, D),
    g1=(1, D),
    s1=(1, D),
    wq=(D, D),
    wk=(D, D),
    wv=(D, D),
    wo=(D, D),
    g2=(1, D),
    s2=(1, D),
    wh=(D, 512),
    bh=(1, 512),
    wr=(512, D),
    br=(1, D),
    dq=(128, D),
    dk=(D, D),
    dv=(D, D),
    do=(D, D),
    wu=(D, 512),
    bu=(1, 512),
    wd=(512, D),
    ps=(1, D),
)


def kernel(*refs):
    gs, *refs = refs
    args, refs = refs[: len(INPUTS)], refs[len(INPUTS) :]
    o_res, o_fg, o_g, *refs = refs
    R = types.SimpleNamespace(**dict(zip([*SCRATCH, *INPUTS], refs, strict=True)))
    G = R.G
    row, col = lax.axis_index("row"), lax.axis_index("col")
    me = row * COLS + col
    core, xbit, ybit = col % 2, (col // 2) % 2, col // 4
    item = me // 2

    def at(number):
        return (number // COLS, number % COLS)

    def remote(src, dst, send, recv, to):
        copy = pltpu.make_async_remote_copy(
            src_ref=src, dst_ref=dst, send_sem=send, recv_sem=recv, device_id=to, device_id_type=MESH
        )
        copy.start()
        return copy

    def drain(ref, sem):
        pltpu.make_async_copy(ref, ref, sem).wait()

    def send_or_copy(src, dst, send, recv, number):
        @pl.when(number != me)
        def _():
            remote(src, dst, send, recv, at(number))

        @pl.when(number == me)
        def _():
            pltpu.make_async_copy(src, dst, recv).start()

    loads = {}
    for i, n in enumerate(INPUTS):
        loads[n] = pltpu.make_async_copy(args[i], getattr(R, n), R.s_in.at[i])
        loads[n].start()

    def need(*wanted):
        for n in wanted:
            loads.pop(n).wait()

    barrier = pltpu.get_barrier_semaphore()
    for k in range(1, DEVICES):
        pl.semaphore_signal(
            barrier, inc=1, device_id=at((me + k) % DEVICES), device_id_type=MESH
        )

    need("fld")
    for ch in range(4):
        R.FA[pl.ds(ch, ITEMS, stride=8), pl.ds(0, 64)] = jnp.transpose(R.fld[:, ch, :])
    size_r, size_c = gs[0, item], gs[1, item]
    fr, fc = size_r.astype(f32), size_c.astype(f32)

    def rotary_tables():
        shape = (80, 128)
        k, lane = iota(shape, 0), iota(shape, 1)
        is_x = k < 16
        coord = jnp.where(
            is_x,
            ((16 * core + k).astype(f32) + 0.5) / fr,
            ((k - 16).astype(f32) + 0.5) / fc,
        )
        freq = (lane % 8 + 1).astype(f32)
        quarter = (lane // 8) % 4
        keep = is_x == (quarter < 2)
        turns = freq * coord
        turns = turns - jnp.round(turns)
        cos_t = jnp.where(keep, turn_sin(turns + 0.25), 0.0)
        sin_t = jnp.where(keep, turn_sin(turns), 0.0)
        sin_t = jnp.where(quarter % 2 == 0, -sin_t, sin_t)
        p, t = iota((PTS, 80), 0), iota((PTS, 80), 1)
        pick = (t == 8 * (p // 512) + (p // 8) % 8) | (t - 16 == 8 * ((p // 64) % 8) + p % 8)
        R.rot[...] = dot_mark(
            pick.astype(jnp.bfloat16), jnp.concatenate([cos_t, sin_t], axis=1), 1
        )

    def fourier_tables():
        shape = (96, 128)
        k, lane = iota(shape, 0), iota(shape, 1)
        is_x = k < 32
        coord = jnp.where(is_x, (k.astype(f32) + 0.5) / fr, ((k - 32).astype(f32) + 0.5) / fc)
        turns = 0.5 * ((lane % 32 + 1).astype(f32) * coord)
        turns = turns - jnp.round(turns)
        turns = jnp.where((lane // 32) % 2 == 0, turns, turns + 0.25)
        R.FF[...] = jnp.where(is_x == (lane < 64), turn_sin(turns), 0.0)

    def tile_masks():
        p = iota((PTS, 128), 0)
        here_r = 16 * core + 8 * (p // 512) + (p // 8) % 8
        here_c = 8 * ((p // 64) % 8) + p % 8
        inv_points = 1.0 / (fr * fc)
        R.wgt[...] = jnp.where((here_r < size_r) & (here_c < size_c), inv_points, 0.0)
        for b in range(ITEMS):
            p = iota((64, 128), 0)
            ok = (NT * row + (p // 8) % 8 < gs[0, b]) & (NT * col + p % 8 < gs[1, b])
            R.mask[pl.ds(64 * b, 64)] = ok.astype(f32)
        p, t = iota((PTS, D), 0), iota((PTS, D), 1)
        chosen = (p // 64 == t // 16) & (
            ((t % 16) == (p // 8) % 8) | ((t % 16) == 8 + p % 8)
        )
        R.E[...] = chosen.astype(jnp.bfloat16)

    rotary_tables()
    fourier_tables()
    tile_masks()
    need("ct", "wd")
    mask2 = jnp.concatenate([R.mask[...]] * 2, axis=1)
    R.ctm[...] = R.ct[...] * mask2
    need("wc")
    R.W9[...] = jnp.zeros((72, D), f32)
    for k in range(9):
        R.W9[pl.ds(8 * k, 4)] = R.wc[k]
    pl.semaphore_wait(barrier, DEVICES - 1)

    for k in range(1, DEVICES):
        to = (me + k) % DEVICES
        remote(
            R.FA.at[pl.ds((to // 2) * 8, 4)],
            R.FR.at[pl.ds(me * 8, 4)],
            R.s_f.at[0],
            R.r_f.at[0],
            at(to),
        )
    R.FR[pl.ds(me * 8, 4)] = R.FA[pl.ds(item * 8, 4)]

    def cossin():
        c, s = R.rot[:, :128], R.rot[:, 128:]
        return jnp.concatenate([c, c], axis=1), jnp.concatenate([s, s], axis=1)

    def turn(v):
        c, s = cossin()
        return v * c + swap_pairs(v) * s

    def turn_back(v):
        c, s = cossin()
        return v * c - swap_pairs(v) * s

    def wgt2():
        return jnp.concatenate([R.wgt[...]] * 2, axis=1)

    need(*list(loads))
    R.FQ[...] = nn(R.FF[...], R.dq[...])
    drain(R.FR.at[pl.ds(0, 4 * (DEVICES - 1))], R.r_f.at[0])
    lane, sub = iota((8, DEVICES * 64), 1), iota((8, DEVICES * 64), 0)
    full_r, full_c = 8 * (lane // 512) + (lane // 8) % 8, 8 * ((lane // 64) % 8) + lane % 8
    full_mask = (full_r < size_r) & (full_c < size_c) & (sub < 4)
    low = iota((8, 128), 1) < 64
    pieces = []
    for k in range(DEVICES // 2):
        left = R.FR[pl.ds(16 * k, 8)]
        right = R.FR[pl.ds(16 * k + 8, 8)]
        pieces.append(jnp.where(low, left, pltpu.roll(right, 64, 1)))
    field = jnp.where(full_mask, jnp.concatenate(pieces, axis=1), 0.0)
    for dj in range(3):
        along = shift_cols(field, dj - 1)
        for di in range(3):
            patch = shift_rows(along, di - 1)
            mine = jnp.where(core == 0, patch[:, :PTS], patch[:, PTS:])
            R.PT[pl.ds((di * 3 + dj) * 8, 8)] = mine

    hidden0 = tn(R.PT[...], R.W9[...]) + R.cb[...]
    R.h0[...] = hidden0
    mean = jnp.mean(hidden0, axis=-1, keepdims=True)
    center = hidden0 - mean
    rstd1 = lax.rsqrt(jnp.mean(center * center, axis=-1, keepdims=True) + 1e-5)
    R.rs1[...] = jnp.broadcast_to(rstd1, (PTS, 128))
    R.n1[...] = center * rstd1
    R.n[...] = R.n1[...] * R.g1[...] + R.s1[...]
    R.k[...] = turn(nn(R.n[...], R.wk[...]))
    R.wn[...] = R.n[...] * wgt2()
    R.T[...] = tn(R.k[...], R.wn[...])

    pair = (row, col + 1 - 2 * core)

    def swap_start(i, value):
        R.XS[i] = value
        return remote(R.XS.at[i], R.XR.at[i], R.s_x.at[i], R.r_x.at[i], pair)

    def swap_end(i, copy):
        copy.wait()
        return R.XS[i] + R.XR[i]

    going = swap_start(0, compact(nn(R.T[...], R.wv[...])))
    R.q[...] = turn(nn(R.n[...], R.wq[...]))
    R.KV[...] = expand(swap_end(0, going))
    R.KVO[...] = nn(R.KV[...], R.wo[...])
    hidden1 = R.h0[...] + nn(R.q[...], R.KVO[...])
    mean = jnp.mean(hidden1, axis=-1, keepdims=True)
    center = hidden1 - mean
    rstd2 = lax.rsqrt(jnp.mean(center * center, axis=-1, keepdims=True) + 1e-5)
    R.rs2[...] = jnp.broadcast_to(rstd2, (PTS, 128))
    R.m1[...] = center * rstd2
    R.m[...] = R.m1[...] * R.g2[...] + R.s2[...]
    R.h1[...] = hidden1 + R.br[...]
    z = nn(R.m[...], R.wh[...]) + R.bh[...]
    R.az[...] = z
    R.a[...] = jax.nn.gelu(z, approximate=True)
    R.h2[...] = R.h1[...] + nn(R.a[...], R.wr[...])
    R.gram[...] = tn(R.h2[...], R.h2[...] * wgt2())
    half = nn(tn(R.dk[...], R.gram[...]), R.dv[...])
    going = swap_start(1, compact(half))
    R.DS[...] = expand(swap_end(1, going))
    R.AB[...] = nn(nn(R.FQ[...], R.DS[...]), R.do[...])

    for k in range(16):
        R.TS[k, pl.ds(0, 8)] = R.AB[pl.ds(16 * core + 8 * (k // 8), 8)]
        R.TS[k, pl.ds(8, 8)] = R.AB[pl.ds(32 + 8 * (k % 8), 8)]
    for k in range(16):
        slot = (me + k) % 16
        send_or_copy(
            R.TS.at[slot],
            R.TR.at[item],
            R.s_t.at[0],
            R.r_t.at[item],
            16 * core + slot,
        )
    R.dact[...] = nt(R.ctm[...], R.wd[...])
    R.rcc[...] = dot_mark(R.E[...], R.ctm[...], 0)
    ps_grad = colsum(R.ctm[...])
    R.az[...] = gelu_both(R.az[...])[1]
    R.X2[...] = nn(R.gram[...], R.dv[...])
    R.P1[...] = nn(R.dq[...], R.DS[...])
    for b in range(ITEMS):
        drain(R.TR.at[b], R.r_t.at[b])

    first, second = (
        xbit * (1 - core) + ybit * core,
        ybit * (1 - core) + xbit * core,
    )
    step_x, step_y = 2 - 4 * xbit, 4 - 8 * ybit
    col_first = col + step_x * (1 - core) + step_y * core
    col_second = col + step_y * (1 - core) + step_x * core

    def sum_chunk(i):
        o, n, kind = CHUNKS[i]
        buf, used, free = R.RB, [SEMS * i], [o]
        place = 2 * ybit + xbit
        half_at = o + core * (n // 2)
        quarter_at = half_at + first * (n // 4)
        eighth_at = quarter_at + second * (n // 8) if kind == AXES else half_at + place * (n // 8)
        shard_at = eighth_at + row * (n // 32)
        plane = [
            (row, col + step_x, 2 * ybit + 1 - xbit),
            (row, col + step_y, 2 * (1 - ybit) + xbit),
            (row, col + step_x + step_y, 2 * (1 - ybit) + 1 - xbit),
        ]
        here = (row, col, place)
        line = [((row + z) % ROWS, col) for z in range(1, ROWS)]

        def part(ref, start, count):
            return ref.at[pl.ds(pl.multiple_of(start, 8), count)]

        def go(src, dst, to):
            copy = remote(src, dst, R.s_g.at[used[0]], R.r_g.at[used[0]], to)
            used[0] += 1
            return copy

        def give(mine, count, *away):
            copies, came = [], []
            for start, to in away:
                here = buf.at[pl.ds(free[0], count)]
                free[0] += count
                came.append(here)
                copies.append(go(part(G, start, count), here, to))

            def add(into):
                for copy in copies:
                    copy.wait()
                total = part(G, mine, count)[...]
                for here in came:
                    total = total + here[...]
                part(into, mine, count)[...] = total

            return add

        def spread(mine, count, *to):
            rows = part(R.SUM, mine, count)
            copies = [go(rows, rows, device) for device in to]

            def wait():
                for copy in copies:
                    copy.wait()

            return wait

        add = give(half_at, n // 2, (o + (1 - core) * (n // 2), pair))
        yield
        add(G)
        if kind == ALL:
            chips = [((row + z) % ROWS, c, p) for z in range(ROWS) for _, c, p in [here, *plane]][1:]
            away = [(half_at + (4 * p + r) * (n // 32), (r, c)) for r, c, p in chips]
            shard_at = half_at + (4 * place + row) * (n // 32)
            add = give(shard_at, n // 32, *away)
            yield
            add(R.SUM)
            wait = spread(shard_at, n // 32, *[(r, c) for r, c, _ in chips])
            yield
            wait()
        elif kind == PLANE:
            away = [(half_at + p * (n // 8), (r, c)) for r, c, p in plane]
            add = give(eighth_at, n // 8, *away)
            yield
            add(G)
        else:
            away = half_at + (1 - first) * (n // 4)
            add = give(quarter_at, n // 4, (away, (row, col_first)))
            yield
            add(G)
            away = quarter_at + (1 - second) * (n // 8)
            add = give(eighth_at, n // 8, (away, (row, col_second)))
            yield
            add(G)
        if kind != ALL:
            away = [(eighth_at + to[0] * (n // 32), to) for to in line]
            add = give(shard_at, n // 32, *away)
            yield
            add(R.SUM)
            wait = spread(shard_at, n // 32, *line)
            yield
            wait()
        if kind == PLANE:
            wait = spread(eighth_at, n // 8, *[(r, c) for r, c, _ in plane])
            yield
            wait()
        elif kind == AXES:
            wait = spread(eighth_at, n // 8, (row, col_second))
            yield
            wait()
            wait = spread(quarter_at, n // 4, (row, col_first))
            yield
            wait()
        wait = spread(half_at, n // 2, pair)
        yield
        wait()
        out = pltpu.make_async_copy(
            R.SUM.at[pl.ds(o, n)], o_g.at[pl.ds(o, n)], R.s_o.at[1 + i]
        )
        out.start()
        outs.append(out)

    going_on, outs, plan = {}, [], list(PLAN)

    def launch(*ready):
        for i, chunk in enumerate(CHUNKS):
            if chunk[0] in ready:
                going_on[i] = sum_chunk(i)
                next(going_on[i])
        step()

    def advance(i):
        if next(going_on[i], i) == i:
            del going_on[i]

    def step():
        for i in plan.pop(0):
            advance(i)

    table = R.TR[...].reshape(ITEMS * 16, D)
    R.UT[...] = nn(table, R.wu[...])
    a, slope = gelu_both(dot_mark(R.E[...], R.UT[...], 1) + R.bu[...])
    R.act[...] = a
    R.dpre[...] = slope * R.dact[...]
    R.rc[...] = dot_mark(R.E[...], R.dpre[...], 0)
    R.DAB[...] = (nt(R.rc[...], R.wu[...]) + R.rcc[...]).reshape(ITEMS, 16, D)
    for k in range(ITEMS):
        b = (item + k) % ITEMS
        send_or_copy(
            R.DAB.at[b],
            R.DR.at[me % 16],
            R.s_r.at[0],
            R.r_r.at[me % 16],
            2 * b + row // 2,
        )
    table = R.TR[...].reshape(ITEMS * 16, D)
    grad = tn(table, R.rc[...])
    G[pl.ds(R_UP, D)] = grad[:, :D]
    G[pl.ds(R_UP + D, D)] = grad[:, D:]
    launch(R_UP)
    G[pl.ds(R_DOWN, 512)] = tn(R.act[...], R.ctm[...])
    step()
    launch(R_DOWN)
    latent = dot_mark(R.E[...], table, 1)
    mask2 = jnp.concatenate([R.mask[...]] * 2, axis=1)
    R.res[...] = (latent + nn(R.act[...], R.wd[...]) + R.ps[...]) * mask2
    out_res = pltpu.make_async_copy(R.res, o_res, R.s_o.at[0])
    out_res.start()
    bu_grad = colsum(R.dpre[...])
    step()

    for k in range(16):
        drain(R.DR.at[k], R.r_r.at[k])
    step()
    da = [jnp.zeros((8, D), f32) for _ in range(2)]
    db = []
    for t in range(COLS):
        for s in range(2):
            da[s] = da[s] + R.DR[s * 8 + t, pl.ds(0, 8)]
        db.append(R.DR[t, pl.ds(8, 8)] + R.DR[8 + t, pl.ds(8, 8)])
    zero = jnp.zeros((8, D), f32)
    is0 = core == 0
    dab = jnp.concatenate(
        [
            jnp.where(is0, da[0], zero),
            jnp.where(is0, da[1], zero),
            jnp.where(is0, zero, da[0]),
            jnp.where(is0, zero, da[1]),
            *db,
        ],
        axis=0,
    )
    going = swap_start(2, compact(tn(R.FQ[...], nt(dab, R.do[...]))))
    dm_table = tn(R.FF[...], dab)
    step()
    G[pl.ds(R_DO, D)] = tn(R.P1[...], dm_table)
    R.DP[...] = nt(dm_table, R.do[...])
    step()
    step()
    step()
    dd = expand(swap_end(2, going))
    step()
    y1 = nn(R.dk[...], dd)
    dgram = nt(y1, R.dv[...]) + nt(R.dv[...], y1)
    step()
    R.dh[...] = nn(R.h2[...], dgram) * wgt2()
    step()
    G[pl.ds(R_DK, D)] = nt(R.X2[...], dd)
    G[pl.ds(R_DV, D)] = tn(R.gram[...], y1)
    step()
    launch(R_DO)
    br_grad = colsum(R.dh[...])
    G[pl.ds(R_RET, 512)] = tn(R.a[...], R.dh[...])
    step()
    launch(R_RET)
    R.dz[...] = nt(R.dh[...], R.wr[...]) * R.az[...]
    bh_grad = colsum(R.dz[...])
    step()
    grad = tn(R.m[...], R.dz[...])
    G[pl.ds(R_HID, D)] = grad[:, :D]
    G[pl.ds(R_HID + D, D)] = grad[:, D:]
    step()
    launch(R_HID)
    dm = nt(R.dz[...], R.wh[...])
    step()
    g2_grad, s2_grad = colsum(dm * R.m1[...]), colsum(dm)
    rs2 = jnp.concatenate([R.rs2[...]] * 2, axis=1)
    R.dh[...] = R.dh[...] + norm_back(dm * R.g2[...], R.m1[...], rs2)
    step()
    stat = tn(R.q[...], R.dh[...])
    going = swap_start(3, compact(nt(stat, R.wo[...])))
    step()
    G[pl.ds(R_O, D)] = tn(R.KV[...], stat)
    R.dq0[...] = turn_back(nt(R.dh[...], R.KVO[...]))
    step()
    G[pl.ds(R_Q, D)] = tn(R.n[...], R.dq0[...])
    step()
    launch(R_O, R_Q)
    dkv = expand(swap_end(3, going))
    G[pl.ds(R_V, D)] = tn(R.T[...], dkv)
    step()
    launch(R_V)
    dt = nt(dkv, R.wv[...])
    R.dk0[...] = turn_back(nt(R.wn[...], dt))
    step()
    G[pl.ds(R_K, D)] = tn(R.n[...], R.dk0[...])
    step()
    launch(R_K)
    dn = (
        nn(R.k[...], dt) * wgt2()
        + nt(R.dq0[...], R.wq[...])
        + nt(R.dk0[...], R.wk[...])
    )
    step()
    g1_grad, s1_grad = colsum(dn * R.n1[...]), colsum(dn)
    rs1 = jnp.concatenate([R.rs1[...]] * 2, axis=1)
    R.dh[...] = R.dh[...] + norm_back(dn * R.g1[...], R.n1[...], rs1)
    step()

    cb_grad = colsum(R.dh[...])
    conv_grad = nn(R.PT[...], R.dh[...])
    vectors = [
        cb_grad, g1_grad, s1_grad, g2_grad, s2_grad, br_grad, ps_grad,
        bh_grad[:, :D], bh_grad[:, D:], bu_grad[:, :D], bu_grad[:, D:],
    ]
    vectors.append(jnp.zeros((128 - S_VEC - len(vectors), D), f32))
    G[pl.ds(R_SMALL, 128)] = jnp.concatenate([conv_grad, *vectors], axis=0)
    G[pl.ds(R_DQ, 128)] = nt(R.DP[...], R.DS[...])
    launch(R_DQ)
    dpt = nt(R.W9[...], R.dh[...])
    half_lane = iota((8, 2 * PTS), 1) // PTS == core
    back = jnp.zeros((8, 2 * PTS), f32)
    for di in range(3):
        line = jnp.zeros((8, 2 * PTS), f32)
        for dj in range(3):
            part = dpt[(di * 3 + dj) * 8 : (di * 3 + dj) * 8 + 8]
            part = jnp.where(half_lane, jnp.concatenate([part, part], axis=1), 0.0)
            line = line + shift_cols(part, 1 - dj)
        back = back + shift_rows(line, 1 - di)
    back = jnp.where(full_mask, back, 0.0)
    for k in range(DEVICES // 2):
        R.FS[pl.ds(8 * k, 8)] = back[:, 128 * k : 128 * (k + 1)]
    for k in range(1, DEVICES):
        to = (me + k) % DEVICES
        remote(
            R.FS.at[pl.ds((to // 2) * 8, 4)],
            R.FB.at[pl.ds(me * 8, 4)],
            R.s_b.at[0],
            R.r_b.at[0],
            at(to),
        )
    R.FB[pl.ds(me * 8, 4)] = R.FS[pl.ds(item * 8, 4)]
    step()

    def field_end():
        drain(R.FB.at[pl.ds(0, 4 * (DEVICES - 1))], R.r_b.at[0])
        for b in range(ITEMS):
            both = R.FB[pl.ds(16 * b, 8)] + R.FB[pl.ds(16 * b + 8, 8)]
            R.FO[pl.ds(8 * b, 8)] = jnp.where(core == 0, both, pltpu.roll(both, 64, 1))
        out = pltpu.make_async_copy(R.FO, o_fg, R.s_o.at[len(CHUNKS) + 1])
        out.start()
        outs.append(out)

    for i in TAIL:
        if i < 0:
            field_end()
        else:
            advance(i)
    assert not going_on and not plan

    drain(R.FR.at[pl.ds(0, 4 * (DEVICES - 1))], R.s_f.at[0])
    drain(R.FB.at[pl.ds(0, 4 * (DEVICES - 1))], R.s_b.at[0])
    inside_t = core == row // 2

    @pl.when(inside_t)
    def _():
        drain(R.TS.at[pl.ds(0, 15)], R.s_t.at[0])
        drain(R.DAB.at[pl.ds(0, 15)], R.s_r.at[0])

    @pl.when(jnp.logical_not(inside_t))
    def _():
        drain(R.TS, R.s_t.at[0])
        drain(R.DAB, R.s_r.at[0])

    out_res.wait()
    for out in outs:
        out.wait()


def vmem(*shape):
    return pltpu.VMEM(shape, f32)


SCRATCH = dict(
    G=vmem(G_ROWS, D),
    RB=vmem(G_ROWS, D),
    SUM=vmem(G_ROWS, D),
    FA=vmem(ITEMS * 8, 128),
    FR=vmem(DEVICES * 8, 128),
    FS=vmem(ITEMS * 8, 128),
    FB=vmem(DEVICES * 8, 128),
    FO=vmem(ITEMS * 8, 128),
    DP=vmem(128, D),
    FQ=vmem(96, D),
    W9=vmem(72, D),
    XS=vmem(4, HEAD, D),
    XR=vmem(4, HEAD, D),
    TS=vmem(16, 16, D),
    TR=vmem(ITEMS, 16, D),
    DAB=vmem(ITEMS, 16, D),
    DR=vmem(16, 16, D),
    mask=vmem(PTS, 128),
    wgt=vmem(PTS, 128),
    ctm=vmem(PTS, D),
    E=pltpu.VMEM((PTS, D), jnp.bfloat16),
    dact=vmem(PTS, 512),
    rcc=vmem(256, D),
    rc=vmem(256, 512),
    rot=vmem(PTS, D),
    FF=vmem(96, 128),
    PT=vmem(72, PTS),
    h0=vmem(PTS, D),
    rs1=vmem(PTS, 128),
    n1=vmem(PTS, D),
    n=vmem(PTS, D),
    wn=vmem(PTS, D),
    q=vmem(PTS, D),
    k=vmem(PTS, D),
    T=vmem(D, D),
    KV=vmem(D, D),
    KVO=vmem(D, D),
    rs2=vmem(PTS, 128),
    m1=vmem(PTS, D),
    m=vmem(PTS, D),
    h1=vmem(PTS, D),
    a=vmem(PTS, 512),
    az=vmem(PTS, 512),
    h2=vmem(PTS, D),
    gram=vmem(D, D),
    DS=vmem(D, D),
    P1=vmem(128, D),
    X2=vmem(D, D),
    AB=vmem(96, D),
    UT=vmem(256, 512),
    act=vmem(PTS, 512),
    dpre=vmem(PTS, 512),
    res=vmem(PTS, D),
    dh=vmem(PTS, D),
    dz=vmem(PTS, 512),
    dq0=vmem(PTS, D),
    dk0=vmem(PTS, D),
    s_in=pltpu.SemaphoreType.DMA((len(INPUTS),)),
    s_f=pltpu.SemaphoreType.DMA((1,)),
    r_f=pltpu.SemaphoreType.DMA((1,)),
    s_b=pltpu.SemaphoreType.DMA((1,)),
    r_b=pltpu.SemaphoreType.DMA((1,)),
    s_t=pltpu.SemaphoreType.DMA((1,)),
    r_t=pltpu.SemaphoreType.DMA((16,)),
    s_r=pltpu.SemaphoreType.DMA((1,)),
    r_r=pltpu.SemaphoreType.DMA((16,)),
    s_x=pltpu.SemaphoreType.DMA((4,)),
    r_x=pltpu.SemaphoreType.DMA((4,)),
    s_g=pltpu.SemaphoreType.DMA((SEMS * len(CHUNKS),)),
    r_g=pltpu.SemaphoreType.DMA((SEMS * len(CHUNKS),)),
    s_o=pltpu.SemaphoreType.DMA((2 + len(CHUNKS),)),
)

PARTS = dict(
    wc=(9, 4, D),
    cb=(1, D),
    g1=(1, D),
    s1=(1, D),
    wq=(D, D),
    wk=(D, D),
    wv=(D, D),
    wo=(D, D),
    g2=(1, D),
    s2=(1, D),
    wh=(D, 512),
    bh=(1, 512),
    wr=(512, D),
    br=(1, D),
    dq=(128, D),
    dk=(D, D),
    dv=(D, D),
    do=(D, D),
    wu=(D, 512),
    bu=(1, 512),
    wd=(512, D),
    ps=(1, D),
)
ROW_AT = dict(
    wq=R_Q, wk=R_K, wv=R_V, wo=R_O, wr=R_RET, dq=R_DQ, dk=R_DK, dv=R_DV, do=R_DO, wd=R_DOWN,
    wh=R_HID, wu=R_UP,
)


SMALL_PARTS = tuple(name for name in PARTS if name not in ROW_AT)


def unpack(res_in, fg_in, g_in, res_out, fg_out, *rest):
    outs = dict(zip(PARTS, rest[: len(PARTS)], strict=True))
    res, fg, g, sem_in, sem_out, fg_here, *here = rest[len(PARTS) :]
    staged = dict(zip(SMALL_PARTS, here, strict=True))
    moves = []

    def add(src, here, *out):
        load = pltpu.make_async_copy(src, here, sem_in.at[len(moves)])
        load.start()
        moves.append((load, out))

    add(g_in.at[pl.ds(R_SMALL, 128)], g.at[pl.ds(R_SMALL, 128)])
    add(fg_in, fg)
    for k in range(4):
        part = pl.ds(k * 256, 256)
        add(res_in.at[part], res.at[part], (res.at[part], res_out.at[part]))
    for name, start in ROW_AT.items():
        count = 512 if name in ("wh", "wu") else PARTS[name][0]
        here = g.at[pl.ds(start, count)]
        if name in ("wh", "wu"):
            out = [
                (g.at[pl.ds(start + s * D, D)], outs[name].at[:, pl.ds(s * D, D)])
                for s in range(2)
            ]
        else:
            out = [(here, outs[name])]
        add(g_in.at[pl.ds(start, count)], here, *out)
    stores = []

    def store(src, dst):
        stores.append(pltpu.make_async_copy(src, dst, sem_out.at[len(stores)]))
        stores[-1].start()

    moves[0][0].wait()
    for k in range(9):
        line = R_SMALL + S_CONV + 8 * k
        staged["wc"][k] = g[line : line + 4]
    line = R_SMALL + S_VEC
    for name in VECS:
        for k in range(PARTS[name][1] // D):
            staged[name][:, D * k : D * (k + 1)] = g[line : line + 1]
            line += 1
    for name in SMALL_PARTS:
        store(staged[name], outs[name])
    moves[1][0].wait()
    for ch in range(4):
        fg_here[:, ch, :] = jnp.transpose(fg[pl.ds(ch, ITEMS, stride=8), pl.ds(0, 64)])
    store(fg_here, fg_out)
    for load, out in moves[2:]:
        load.wait()
        for src, dst in out:
            store(src, dst)
    for out in stores:
        out.wait()


ARGUMENTS = tuple(n for n in INPUTS if n not in ("fld", "ct"))


def item_body(field_in, *rest):
    values = dict(zip(ARGUMENTS + ("ct", "gs"), rest, strict=True))
    values["fld"] = field_in.transpose(1, 2, 3, 0)
    operands = [values["gs"].T]
    operands += [values[name].reshape(shape) for name, shape in INPUTS.items()]
    in_smem = pl.BlockSpec(memory_space=pltpu.SMEM)
    anywhere = pl.BlockSpec(memory_space=pl.ANY)
    made = pl.pallas_call(
        kernel,
        out_shape=(
            jax.ShapeDtypeStruct((PTS, D), f32),
            jax.ShapeDtypeStruct((ITEMS * 8, 128), f32),
            jax.ShapeDtypeStruct((G_ROWS, D), f32),
        ),
        in_specs=[in_smem] + [anywhere] * len(INPUTS),
        out_specs=(anywhere,) * 3,
        scratch_shapes=[*SCRATCH.values()] + [vmem(*shape) for shape in INPUTS.values()],
        compiler_params=pltpu.CompilerParams(
            collective_id=1, has_side_effects=True, vmem_limit_bytes=60 * 2**20
        ),
        name="layer",
    )(*operands)
    outs = pl.pallas_call(
        unpack,
        out_shape=(
            jax.ShapeDtypeStruct((PTS, D), f32),
            jax.ShapeDtypeStruct((NT * NT, 4, ITEMS), f32),
            *(jax.ShapeDtypeStruct(shape, f32) for shape in PARTS.values()),
        ),
        in_specs=[anywhere] * 3,
        out_specs=(anywhere,) * (2 + len(PARTS)),
        scratch_shapes=[
            vmem(PTS, D),
            vmem(ITEMS * 8, 128),
            vmem(G_ROWS, D),
            pltpu.SemaphoreType.DMA((24,)),
            pltpu.SemaphoreType.DMA((40,)),
            vmem(NT * NT, 4, ITEMS),
            *(vmem(*PARTS[name]) for name in SMALL_PARTS),
        ],
        compiler_params=pltpu.CompilerParams(vmem_limit_bytes=60 * 2**20),
        name="unpack",
    )(*made)
    shaped = []
    for name, value in zip(PARTS, outs[2:], strict=True):
        if name == "wc":
            value = value.reshape(3, 3, 4, D)
        elif name in VECS:
            value = value.reshape(-1)
        shaped.append(value)
    return (
        outs[0].reshape(ITEMS, NT, NT, D),
        outs[1].reshape(NT, NT, 4, ITEMS).transpose(3, 0, 1, 2),
        *shaped,
    )


def body(field_in, *rest):
    tile = field_in.shape[:3]
    mesh = (lax.axis_size("row"), lax.axis_size("col"))
    if mesh == (ROWS, COLS) and tile == (ITEMS, NT, NT):
        return item_body(field_in, *rest)
    return general_body(field_in, *rest)


def solution(mesh):
    spread = P(None, "row", "col", None)
    placed = (spread,) + (P(),) * 22 + (spread, P())
    return jax.shard_map(
        body,
        mesh=mesh,
        in_specs=placed,
        out_specs=(spread, spread) + (P(),) * 22,
        check_vma=False,
    )
```
